128 devices in a mesh: frame: 32 (over x, z, y_hi), head: 4 (over y_lo, core).
Axes of the slice: x: 4, y: 4 (y_hi: 2, y_lo: 2; y = y_hi * 2 + y_lo), z: 4, core: 2. Of those that a mesh axis runs over, the one named last changes fastest.
Arguments:
- tokens: bfloat16 [32, 1024, 1280], P('frame', None, 'head')
- norm_gain: float32 [2, 1280], replicated, may hold values from 0.1 to 1.9
- w_qkv: bfloat16 [2, 1280, 3, 1280], P(None, None, None, 'head')
- w_out: bfloat16 [2, 1280, 1280], P(None, None, 'head'), may hold values from -0.5 to 0.5
- out_bias: bfloat16 [2, 1280], P(None, 'head'), may hold values from -3 to 3
Outputs:
- mixed: bfloat16 [32, 1024, 1280], P('frame', None, 'head')
The draws below stay inside these ranges and needn't reach their ends.
All inputs are finite; a program needn't handle non-finite values.
Results may differ from the reference program's by a relative error of at most 0.014.
Values may be sent and summed in bfloat16 or wider, within the bound.
A program may use at most 128 MiB of HBM per device.

```python
import jax
import jax.numpy as jnp
from jax import lax

D = 1280
HEAD_DIM = 64
TOK = 1024
BLOCKS = 2
FRAMES = 32


def draw_tokens(key, part):
    key = jax.random.fold_in(key, 11)
    first = jax.random.fold_in(key, 0)
    values = jax.random.normal(first, (FRAMES, TOK, D))
    return values.astype(jnp.bfloat16)


def draw_w_qkv(key, part):
    key = jax.random.fold_in(key, 23)
    keys_all = jax.random.split(key, 3)
    shape = (BLOCKS, D, 1, D)
    query_part = 1.5 * jax.random.normal(keys_all[0], shape)
    key_part = 1.5 * jax.random.normal(keys_all[1], shape)
    value_part = jax.random.normal(keys_all[2], shape)
    values = jnp.concatenate([query_part, key_part, value_part], 2) * D ** (-0.5)
    return values.astype(jnp.bfloat16)


def shard_levels(own_key, dims, pieces, low, largest):
    gain = 1.0
    for dim, shards_of in pieces:
        draws = jax.random.uniform(jax.random.fold_in(jax.random.fold_in(own_key, 6), dim), (shards_of,), jnp.float32, low / len(pieces), largest / len(pieces))
        gain = gain * jnp.repeat(jnp.exp(draws), dims[dim] // shards_of).reshape((-1,) + (1,) * (len(dims) - 1 - dim))
    return gain


def scatter_about(key, shape, scale, bound, pieces=(), kind=jnp.bfloat16):
    drawn = jax.random.normal(key, shape, jnp.float32) * scale
    if len(pieces) > 0:
        drawn = shard_levels(key, shape, pieces, -0.22, 0.18) * drawn
    return jnp.clip(drawn, min=-bound, max=bound).astype(kind)


def setup_inputs(seed: int = 0) -> dict:
    streams_of = jax.random.split(jax.random.key(seed), 6)
    tokens = draw_tokens(jax.random.fold_in(streams_of[5], 71), 0)
    norm_gain = jnp.clip(1.0 + 0.18 * jax.random.normal(streams_of[1], (BLOCKS, D), jnp.float32), 0.1, 1.9)
    w_qkv = draw_w_qkv(jax.random.fold_in(streams_of[5], 71), 0)
    w_out = scatter_about(streams_of[3], (BLOCKS, D, D), (3 * D ** -0.5), 0.5, ((2, 4),))
    out_bias = scatter_about(streams_of[4], (BLOCKS, D), 0.5, 3.0, ((1, 4),))
    return dict(tokens=tokens, norm_gain=norm_gain, w_qkv=w_qkv, w_out=w_out, out_bias=out_bias)


def normalize(activations, gain_row):
    widened = activations.astype(jnp.float32)
    average = lax.optimization_barrier(jnp.mean(widened, axis=-1, keepdims=True))
    variance = lax.optimization_barrier(jnp.mean((widened - average) ** 2, axis=-1, keepdims=True))
    return ((widened - average) * lax.rsqrt(variance + 1e-05) * gain_row).astype(jnp.bfloat16)

def reference(tokens, norm_gain, w_qkv, w_out, out_bias):
    frames, frame_tokens, width = tokens.shape
    heads_all = width // HEAD_DIM
    scale = HEAD_DIM ** (-0.5)
    current = tokens
    for layer in range(BLOCKS):
        weights_in = w_qkv[layer].reshape(width, 3 * width)
        gain_row = norm_gain[layer]

        def project(frame_rows):
            normed = normalize(frame_rows, gain_row)
            return jnp.dot(normed, weights_in, preferred_element_type=jnp.float32).astype(jnp.bfloat16).reshape(frame_tokens, 3, width)
        projected = lax.map(project, current)
        first_pair = projected[0, :, 1:]
        previous_index = jnp.maximum(jnp.arange(frames) - 1, 0)
        predecessors = projected[previous_index, :, 1:]

        def attend_frame(frame_item):
            query_rows, pair_rows = frame_item
            key_value = jnp.concatenate([first_pair, pair_rows], 0)
            key_rows = key_value[:, 0].reshape(2 * frame_tokens, heads_all, HEAD_DIM).astype(jnp.float32)
            value_rows = key_value[:, 1].reshape(2 * frame_tokens, heads_all, HEAD_DIM).astype(jnp.float32)
            query_heads = query_rows.reshape(frame_tokens, heads_all, HEAD_DIM).astype(jnp.float32)
            scores = jnp.einsum('qhe,khe->hqk', query_heads, key_rows) * scale
            row_max = lax.optimization_barrier(jnp.max(scores, axis=-1, keepdims=True))
            expo = jnp.exp(scores - row_max)
            weights = (expo / lax.optimization_barrier(jnp.sum(expo, axis=-1, keepdims=True))).astype(jnp.bfloat16)
            result = jnp.einsum('hqk,khe->qhe', weights.astype(jnp.float32), value_rows)
            return result.astype(jnp.bfloat16).reshape(frame_tokens, width)
        attended = lax.map(attend_frame, (projected[:, :, 0], predecessors))
        weights_out = w_out[layer]
        bias_row = out_bias[layer].astype(jnp.float32)

        def output(frame_item):
            attended_rows, input_rows = frame_item
            summed = jnp.dot(attended_rows, weights_out, preferred_element_type=jnp.float32)
            return (summed + bias_row + input_rows.astype(jnp.float32)).astype(jnp.bfloat16)
        current = lax.map(output, (attended, current))
    return current
```

```python
import functools

import jax
import jax.numpy as jnp
from jax import lax
from jax.experimental import pallas as pl
from jax.experimental.pallas import tpu as pltpu
from jax.sharding import PartitionSpec as P

HEAD_DIM = 64
BLOCKS = 2
HEADS = 5
CHUNKS = 4
RING = 4
MESH = pl.DeviceIdType.MESH
f32 = jnp.float32
bf16 = jnp.bfloat16
SCALE = HEAD_DIM**-0.5 * 1.4426950408889634


def rcopy(src, dst, send, recv, device):
    return pltpu.make_async_remote_copy(
        src_ref=src,
        dst_ref=dst,
        send_sem=send,
        recv_sem=recv,
        device_id=device,
        device_id_type=MESH,
    )


def kernel(
    tok, gain, w, wo, bias, out,
    xg, x1, wbuf, wo0, bo0, wo1, bo1, q_s, kv, kvp, kv0, attg, att1, res, acc_s, m_s, l_s,
    x_send, xf_send, x_recv, w_send, w_recv, o_send, o_recv, b_send, b_recv,
    kv_send, kv_recv, z_send, z_recv, a_send, af_send, a_recv, h_send, h_recv, r_send, r_recv,
):
    tokens = tok.shape[0]
    qw = tok.shape[1]
    width = gain.shape[1]
    cr = tokens // CHUNKS
    f = lax.axis_index("frame")
    h = lax.axis_index("head")
    k, y, c = f // 2, (f % 2) * 2 + h // 2, h % 2
    x, z = k // RING, k % RING
    frames = lax.axis_size("frame")
    frame = 2 * k + c
    home = y // 2
    rel = (y - 2 * c + RING) % RING
    q_own = (y % 2) * 2 + c
    group = (y % 2) * 2 + y // 2

    def dev(kk, yy, cc):
        return (kk * 2 + yy // 2, (yy % 2) * 2 + cc)

    def plane(dx, dz, cc):
        return dev(((x + dx + RING) % RING) * RING + (z + dz + RING) % RING, y, cc)

    yp, ym = (y + 1) % RING, (y + RING - 1) % RING
    other = dev(k, y, 1 - c)
    ks = frames // 2
    far = dev((k + jnp.where(c == 1, 1, ks - 1)) % ks, y, 1 - c)
    target = dev(((frame + 1) % frames) // 2, y, 1 - c)

    barrier = pltpu.get_barrier_semaphore()
    friends = [
        other, far,
        dev(k, yp, 0), dev(k, yp, 1), dev(k, ym, 0), dev(k, ym, 1),
        plane(1, 0, c), plane(-1, 0, c), plane(0, 1, c), plane(0, -1, c),
    ]
    for d in friends:
        pl.semaphore_signal(barrier, inc=1, device_id=d, device_id_type=MESH)
    pl.semaphore_wait(barrier, len(friends))

    def rows(ch):
        return pl.ds(ch * cr if isinstance(ch, int) else pl.multiple_of(ch * cr, cr), cr)

    def x_send_to(i, ch, device):
        r = rows(ch)
        return rcopy(tok.at[r], xg.at[q_own, r], x_send.at[i, ch], x_recv.at[q_own, ch], device)

    def x_wait(q, ch):
        r = rows(ch)
        rcopy(xg.at[q, r], xg.at[q, r], x_send.at[0, 0], x_recv.at[q, ch], other).wait_recv()

    plus = jnp.logical_or(rel == 1, rel == 2)
    fbase = jnp.where(plus, 0, 2)
    fpair = 2 * (1 - rel % 2)
    fdev = dev(k, jnp.where(plus, yp, ym), c)

    def x_fwd(j, s):
        r = rows(fbase + s)
        qq = fpair + j
        return rcopy(xg.at[qq, r], xg.at[qq, r], xf_send.at[j, s], x_recv.at[qq, fbase + s], fdev)

    def x_local(ch):
        r = rows(ch)
        return pltpu.make_async_copy(tok.at[r], xg.at[q_own, r], x_recv.at[q_own, ch])

    def x_issue(s):
        for first, second in ((s, 2 + s),):
            x_send_to(0, first, dev(k, yp, home)).start()
            x_send_to(1, second, dev(k, ym, home)).start()
            x_send_to(0, second, dev(k, yp, home)).start()
            x_send_to(1, first, dev(k, ym, home)).start()

        @pl.when(c == home)
        def _():
            x_local(s).start()
            x_local(2 + s).start()

        @pl.when(c != home)
        def _():
            x_send_to(2, s, other).start()
            x_send_to(2, 2 + s, other).start()

    x_issue(0)
    x_issue(1)

    for layer in range(BLOCKS):
        @pl.when(c == home)
        def _():
            pltpu.make_async_copy(w.at[layer], wbuf.at[layer], w_recv.at[layer]).start()
            rcopy(w.at[layer], wbuf.at[layer], w_send.at[layer], w_recv.at[layer], other).start()

    def w_wait(layer):
        rcopy(wbuf.at[layer], wbuf.at[layer], w_send.at[0], w_recv.at[layer], other).wait_recv()

    def wo1_copies():
        return (
            rcopy(wo.at[1], wo1.at[c], o_send.at[3], o_recv.at[4 + c], other),
            rcopy(bias.at[1], bo1.at[c], b_send.at[3], b_recv.at[4 + c], other),
        )

    @pl.when(c == home)
    def _():
        pltpu.make_async_copy(wo.at[1], wo1.at[c], o_recv.at[4 + c]).start()
        pltpu.make_async_copy(bias.at[1], bo1.at[c], b_recv.at[4 + c]).start()

    @pl.when(c != home)
    def _():
        for cp in wo1_copies():
            cp.start()

    def wo0_send(i, src_w, src_b, q, device):
        return (
            rcopy(src_w, wo0.at[q], o_send.at[i], o_recv.at[q], device),
            rcopy(src_b, bo0.at[q], b_send.at[i], b_recv.at[q], device),
        )

    def wo0_own():
        return (
            wo0_send(0, wo.at[0], bias.at[0], q_own, other)
            + wo0_send(1, wo.at[0], bias.at[0], q_own, dev(k, ym, c))
        )

    q_next = (yp % 2) * 2 + c

    def wo0_fwd():
        return wo0_send(2, wo0.at[q_next], bo0.at[q_next], q_next, other)

    def wo0_wait(q):
        for cp in wo0_send(0, wo0.at[q], bo0.at[q], q, other):
            cp.wait_recv()

    def ln_qkv(layer, src, ch):
        r = rows(ch)
        xs = [src[q, r, :].astype(f32) for q in range(4)]
        mean = sum(jnp.sum(v, -1, keepdims=True) for v in xs) * (1.0 / width)
        ds = [v - mean for v in xs]
        var = sum(jnp.sum(v * v, -1, keepdims=True) for v in ds) * (1.0 / width)
        inv = lax.rsqrt(var + 1e-5)
        normed = [
            (v * inv * gain[layer : layer + 1, q * qw : (q + 1) * qw]).astype(bf16)
            for q, v in enumerate(ds)
        ]
        proj = jnp.dot(jnp.concatenate(normed, axis=1), wbuf[layer], preferred_element_type=f32)
        for s in range(HEADS):
            kv[layer, s, r, :] = proj[:, 128 * s : 128 * (s + 1)].astype(bf16)
        q_s[r, :] = (proj[:, 640:] * SCALE).astype(bf16)

    def kv_copy(layer, ch):
        r = rows(ch)
        return rcopy(
            kv.at[layer, :, r], kvp.at[layer, :, r],
            kv_send.at[layer, ch], kv_recv.at[layer, ch], target,
        )

    def zcopy(layer, ch, i, src, device):
        r = rows(ch)
        return rcopy(
            src.at[layer, :, r], kv0.at[layer, :, r],
            z_send.at[layer, ch, i], z_recv.at[layer, ch], device,
        )

    def z_targets(ch):
        low = ch < 2
        up = plane(0, 1, c), plane(0, -1, c), plane(1, 0, c), plane(-1, 0, c)
        conds = (
            jnp.logical_or(z == 0, jnp.logical_and(z == 1, low)),
            jnp.logical_or(z == 0, jnp.logical_and(z == 3, jnp.logical_not(low))),
            jnp.logical_and(z == 0, jnp.logical_or(x == 0, jnp.logical_and(x == 1, low))),
            jnp.logical_and(
                z == 0, jnp.logical_or(x == 0, jnp.logical_and(x == 3, jnp.logical_not(low)))
            ),
        )
        return [(i, d, cond) for i, (d, cond) in enumerate(zip(up, conds))]

    def z_forward(layer, ch, src, method):
        for i, d, cond in z_targets(ch):
            @pl.when(cond)
            def _():
                getattr(zcopy(layer, ch, i, src, d), method)()

        getattr(zcopy(layer, ch, 4, src, other), method)()

    def send_kv(layer, ch):
        r = rows(ch)

        @pl.when(frame < frames - 1)
        def _():
            kv_copy(layer, ch).start()

        @pl.when(frame == 0)
        def _():
            pltpu.make_async_copy(
                kv.at[layer, :, r], kv0.at[layer, :, r], z_recv.at[layer, ch]
            ).start()
            z_forward(layer, ch, kv, "start")

    def z_wait(layer, ch):
        zcopy(layer, ch, 4, kv0, other).wait_recv()

    def relay(layer):
        @pl.when(jnp.logical_and(c == 0, frame > 0))
        def _():
            def body(i, carry):
                ch = (i % 2) * 2 + i // 2
                z_wait(layer, ch)
                z_forward(layer, ch, kv0, "start")
                return carry

            lax.fori_loop(0, CHUNKS, body, 0)

    def relay_end(layer):
        @pl.when(jnp.logical_or(c == 1, frame == 0))
        def _():
            for ch in range(CHUNKS):
                z_wait(layer, ch)

    lane = lax.broadcasted_iota(jnp.int32, (cr, 128), 1)
    ones = jnp.ones((tokens, 128), bf16)

    def half(head, r, keys, layer):
        p, s = head // 2, head % 2
        qq = q_s[r, 128 * p : 128 * (p + 1)]
        if head < 4:
            qq = jnp.where((lane // 64) == s, qq, jnp.zeros_like(qq))
            ks_, vs_ = 2 * p, 2 * p + 1
        else:
            ks_, vs_ = 4, 4
        scores = lax.dot_general(
            qq, keys[layer, ks_], (((1,), (1,)), ((), ())), preferred_element_type=f32
        )
        values = jnp.concatenate([keys[layer, vs_], ones], axis=1)
        return scores, values

    def part1(layer):
        @pl.when(frame > 0)
        def _():
            for ch in range(CHUNKS):
                kv_copy(layer, ch).wait_recv()

            def body(ch, carry):
                r = rows(ch)
                for head in range(HEADS):
                    scores, values = half(head, r, kvp, layer)
                    top = jnp.max(scores, -1, keepdims=True)
                    e = jnp.exp2(scores - top).astype(bf16)
                    o = jnp.dot(e, values, preferred_element_type=f32)
                    acc_s[head, r, :] = o[:, :128]
                    l_s[head, r, :] = o[:, 128:]
                    m_s[head, r, :] = jnp.broadcast_to(top, (cr, 128))
                return carry

            lax.fori_loop(0, CHUNKS, body, 0)

        @pl.when(frame == 0)
        def _():
            def body(ch, carry):
                r = rows(ch)
                for head in range(HEADS):
                    acc_s[head, r, :] = jnp.zeros((cr, 128), f32)
                    l_s[head, r, :] = jnp.zeros((cr, 128), f32)
                    m_s[head, r, :] = jnp.full((cr, 128), -jnp.inf, f32)
                return carry

            lax.fori_loop(0, CHUNKS, body, 0)

    def part2(layer, ch, store):
        r = rows(ch)
        pieces = []
        for head in range(HEADS):
            scores, values = half(head, r, kv0, layer)
            before = m_s[head, r, :]
            top = jnp.maximum(before, jnp.max(scores, -1, keepdims=True))
            wide = jnp.concatenate([top] * (tokens // 128), axis=1)
            e = jnp.exp2(scores - wide).astype(bf16)
            o = jnp.dot(e, values, preferred_element_type=f32)
            alpha = jnp.exp2(before - top)
            total = l_s[head, r, :] * alpha + o[:, 128:]
            pieces.append((acc_s[head, r, :] * alpha + o[:, :128]) / total)
        store(r, 0, jnp.where(lane < 64, pieces[0], pieces[1]).astype(bf16))
        store(r, 1, jnp.where(lane < 64, pieces[2], pieces[3]).astype(bf16))
        store(r, 2, pieces[4][:, :64].astype(bf16))

    def order(i):
        return (i % 2) * 2 + i // 2

    g_m = (ym % 2) * 2 + ym // 2
    g_p = (yp % 2) * 2 + yp // 2
    g_o = (((y + 2) % RING) % 2) * 2 + ((y + 2) % RING) // 2

    for s in range(2):
        x_wait(fpair, fbase + s)
        x_wait(fpair + 1, fbase + s)
        x_fwd(0, s).start()
        x_fwd(1, s).start()
    for s in range(2):
        x_wait(fpair, 2 - fbase + s)
        x_wait(fpair + 1, 2 - fbase + s)
        for j in range(2):
            x_wait(2 - fpair + j, s)
            x_wait(2 - fpair + j, 2 + s)

    w_wait(0)

    def first(i, carry):
        ch = order(i)
        ln_qkv(0, xg, ch)
        send_kv(0, ch)
        return carry

    lax.fori_loop(0, CHUNKS, first, 0)

    pltpu.make_async_copy(wo.at[0], wo0.at[q_own], o_recv.at[q_own]).start()
    pltpu.make_async_copy(bias.at[0], bo0.at[q_own], b_recv.at[q_own]).start()
    for cp in wo0_own():
        cp.start()

    relay(0)
    part1(0)
    relay_end(0)

    wo0_wait(q_next)
    for cp in wo0_fwd():
        cp.start()

    def a_copy(direction, ch):
        r = rows(ch)
        return rcopy(
            attg.at[group, r], attg.at[group, r], a_send.at[direction, ch],
            a_recv.at[group, ch], dev(k, yp if direction == 0 else ym, c),
        )

    def a_fwd(direction, s):
        ch = s if direction == 0 else 2 + s
        g = g_m if direction == 0 else g_p
        r = rows(ch)
        return rcopy(
            attg.at[g, r], attg.at[g, r], af_send.at[direction, s],
            a_recv.at[g, ch], dev(k, yp if direction == 0 else ym, c),
        )

    def a_wait(g, ch):
        r = rows(ch)
        rcopy(attg.at[g, r], attg.at[g, r], a_send.at[0, 0], a_recv.at[g, ch], other).wait_recv()

    def a_forward(s):
        a_wait(g_m, s)
        a_fwd(0, s).start()
        a_wait(g_p, 2 + s)
        a_fwd(1, s).start()

    def store0(r, p, v):
        attg[group, r, 128 * p : 128 * p + v.shape[1]] = v

    def second0(i, carry):
        ch = order(i)
        part2(0, ch, store0)
        a_copy(0, ch).start()
        a_copy(1, ch).start()

        @pl.when(i == 2)
        def _():
            a_forward(0)

        return carry

    lax.fori_loop(0, CHUNKS, second0, 0)
    wo0_wait(q_own)
    wo0_wait((y % 2) * 2 + 1 - c)
    wo0_wait((yp % 2) * 2 + 1 - c)
    w_wait(1)

    def project(ch):
        r = rows(ch)
        attended = jnp.concatenate([attg[g, r, :] for g in range(4)], axis=1)
        for q in range(4):
            summed = jnp.dot(attended, wo0[q], preferred_element_type=f32)
            x1[q, r, :] = (summed + bo0[q, 0:1, :] + xg[q, r, :].astype(f32)).astype(bf16)
        ln_qkv(1, x1, ch)
        send_kv(1, ch)

    a_forward(1)

    def third(i, carry):
        @pl.when(i % 2 == 0)
        def _():
            s = i // 2
            a_wait(g_m, 2 + s)
            a_wait(g_p, s)
            a_wait(g_o, s)
            a_wait(g_o, 2 + s)

        project(order(i))
        return carry

    lax.fori_loop(0, CHUNKS, third, 0)

    relay(1)
    part1(1)
    relay_end(1)

    at_home = rel < 2
    mate = dev(k, jnp.where(rel == 0, yp, ym), c)
    near = dev(k, jnp.where(rel == 2, ym, yp), c)
    g_near = jnp.where(rel == 0, g_m, g_p)
    g_mate = jnp.where(rel == 0, g_p, g_m)

    def h_copy(ch, device):
        r = rows(ch)
        return rcopy(
            att1.at[group, r], att1.at[group, r], h_send.at[0, ch], h_recv.at[group, ch], device
        )

    def h_fwd(ch):
        r = rows(ch)
        return rcopy(
            att1.at[g_near, r], att1.at[g_near, r], h_send.at[1, ch], h_recv.at[g_near, ch], mate
        )

    def h_wait(g, ch):
        r = rows(ch)
        rcopy(att1.at[g, r], att1.at[g, r], h_send.at[0, 0], h_recv.at[g, ch], other).wait_recv()

    def store1(r, p, v):
        att1[group, r, 128 * p : 128 * p + v.shape[1]] = v

    def second1(i, carry):
        ch = order(i)
        part2(1, ch, store1)

        @pl.when(at_home)
        def _():
            h_copy(ch, mate).start()

        @pl.when(jnp.logical_not(at_home))
        def _():
            h_copy(ch, near).start()

        return carry

    lax.fori_loop(0, CHUNKS, second1, 0)

    def r_copy(ch):
        r = rows(ch)
        return rcopy(res.at[1 - c, r], out.at[r], r_send.at[ch], r_recv.at[ch], other)

    @pl.when(at_home)
    def _():
        for j in range(2):
            rcopy(wo.at[1], wo1.at[j], o_send.at[0], o_recv.at[4 + j], other).wait_recv()
            rcopy(bias.at[1], bo1.at[j], b_send.at[0], b_recv.at[4 + j], other).wait_recv()

        def forward(i, carry):
            ch = order(i)
            h_wait(g_near, ch)
            h_fwd(ch).start()
            return carry

        lax.fori_loop(0, CHUNKS, forward, 0)

        def last(i, carry):
            ch = order(i)
            r = rows(ch)
            h_wait(g_mate, ch)
            h_wait(g_o, ch)
            attended = jnp.concatenate([att1[g, r, :] for g in range(4)], axis=1)
            for j in range(2):
                summed = jnp.dot(attended, wo1[j], preferred_element_type=f32)
                total = summed + bo1[j, 0:1, :] + x1[(y % 2) * 2 + j, r, :].astype(f32)
                res[j, r, :] = total.astype(bf16)
            r_copy(ch).start()
            out[r, :] = res[c, r, :]
            return carry

        lax.fori_loop(0, CHUNKS, last, 0)
        for ch in range(CHUNKS):
            r_copy(ch).wait_send()
            h_copy(ch, mate).wait_send()
            h_fwd(ch).wait_send()

    @pl.when(jnp.logical_not(at_home))
    def _():
        for ch in range(CHUNKS):
            h_copy(ch, near).wait_send()
            r_copy(ch).wait_recv()

    for s in range(2):
        for j in range(2):
            x_fwd(j, s).wait_send()
            a_fwd(j, s).wait_send()
    for ch in range(CHUNKS):
        x_send_to(0, ch, other).wait_send()
        x_send_to(1, ch, other).wait_send()
        a_copy(0, ch).wait_send()
        a_copy(1, ch).wait_send()
    for cp in wo0_own() + wo0_fwd():
        cp.wait_send()

    @pl.when(c == home)
    def _():
        for layer in range(BLOCKS):
            rcopy(w.at[layer], wbuf.at[layer], w_send.at[layer], w_recv.at[layer], other).wait_send()

    @pl.when(c != home)
    def _():
        for cp in wo1_copies():
            cp.wait_send()
        for ch in range(CHUNKS):
            x_send_to(2, ch, other).wait_send()

    for layer in range(BLOCKS):
        @pl.when(frame < frames - 1)
        def _():
            for ch in range(CHUNKS):
                kv_copy(layer, ch).wait_send()

        @pl.when(c == 0)
        def _():
            for ch in range(CHUNKS):
                z_forward(layer, ch, kv0, "wait_send")


def arrange(w_qkv):
    q, kk, v = w_qkv[:, :, 0], w_qkv[:, :, 1], w_qkv[:, :, 2]
    gap = jnp.zeros(q.shape[:2] + (HEAD_DIM,), q.dtype)
    return jnp.concatenate(
        [
            kk[..., :128], v[..., :128], kk[..., 128:256], v[..., 128:256],
            v[..., 256:], kk[..., 256:], q[..., :256], gap, q[..., 256:],
        ],
        axis=-1,
    )


def shards(tokens, norm_gain, w_qkv, w_out, out_bias):
    rows, qw = tokens.shape[1:]
    width = w_qkv.shape[1]
    cols = 1024
    w = arrange(w_qkv)
    bias = jnp.broadcast_to(out_bias.astype(f32)[:, None, :], (BLOCKS, 8, qw))
    any_spec = pl.BlockSpec(memory_space=pl.ANY)
    vmem = pl.BlockSpec(memory_space=pltpu.VMEM)
    dma = pltpu.SemaphoreType.DMA
    result = pl.pallas_call(
        kernel,
        out_shape=jax.ShapeDtypeStruct((rows, qw), bf16),
        in_specs=[any_spec, vmem, any_spec, any_spec, any_spec],
        out_specs=vmem,
        scratch_shapes=[
            pltpu.VMEM((4, rows, qw), bf16),
            pltpu.VMEM((4, rows, qw), bf16),
            pltpu.VMEM((BLOCKS, width, cols), bf16),
            pltpu.VMEM((4, width, qw), bf16),
            pltpu.VMEM((4, 8, qw), f32),
            pltpu.VMEM((2, width, qw), bf16),
            pltpu.VMEM((2, 8, qw), f32),
            pltpu.VMEM((rows, 384), bf16),
            pltpu.VMEM((BLOCKS, HEADS, rows, 128), bf16),
            pltpu.VMEM((BLOCKS, HEADS, rows, 128), bf16),
            pltpu.VMEM((BLOCKS, HEADS, rows, 128), bf16),
            pltpu.VMEM((4, rows, qw), bf16),
            pltpu.VMEM((4, rows, qw), bf16),
            pltpu.VMEM((2, rows, qw), bf16),
            pltpu.VMEM((HEADS, rows, 128), f32),
            pltpu.VMEM((HEADS, rows, 128), f32),
            pltpu.VMEM((HEADS, rows, 128), f32),
            dma((3, CHUNKS)), dma((2, 2)), dma((4, CHUNKS)), dma((2,)), dma((2,)),
            dma((4,)), dma((6,)), dma((4,)), dma((6,)),
            dma((BLOCKS, CHUNKS)), dma((BLOCKS, CHUNKS)),
            dma((BLOCKS, CHUNKS, 5)), dma((BLOCKS, CHUNKS)),
            dma((2, CHUNKS)), dma((2, 2)), dma((4, CHUNKS)),
            dma((2, CHUNKS)), dma((4, CHUNKS)), dma((CHUNKS,)), dma((CHUNKS,)),
        ],
        compiler_params=pltpu.CompilerParams(
            collective_id=0, has_side_effects=True, vmem_limit_bytes=60 << 20
        ),
        name="video_blocks",
    )(tokens[0], norm_gain, w, w_out, bias)
    return result[None]


def solution(mesh):
    placed = (
        P("frame", None, "head"),
        P(),
        P(None, None, None, "head"),
        P(None, None, "head"),
        P(None, "head"),
    )
    return jax.shard_map(
        shards, mesh=mesh, in_specs=placed, out_specs=P("frame", None, "head"), check_vma=False
    )
```

```python
import functools

import jax
import jax.numpy as jnp
from jax import lax
from jax.experimental import pallas as pl
from jax.experimental.pallas import tpu as pltpu
from jax.sharding import PartitionSpec as P

HEAD_DIM = 64
BLOCKS = 2
HEADS = 5
CHUNKS = 8
STEPS = 4
HALVES = 2
RING = 4
MESH = pl.DeviceIdType.MESH
f32 = jnp.float32
bf16 = jnp.bfloat16
SCALE = HEAD_DIM**-0.5 * 1.4426950408889634


def rcopy(src, dst, send, recv, device):
    return pltpu.make_async_remote_copy(
        src_ref=src,
        dst_ref=dst,
        send_sem=send,
        recv_sem=recv,
        device_id=device,
        device_id_type=MESH,
    )


def kernel(
    tok, gain, w, wo, bias, out,
    xg, x1, wbuf, wo0, bo0, wo1, bo1, q_s, kv, kvp, kv0, attg, att1, res, acc_s, m_s, l_s, gcol, bcol,
    x_send, xf_send, x_recv, w_send, w_recv, o_send, o_recv, b_send, b_recv,
    kv_send, kv_recv, q_send, q_recv, d_send, z_send, z_recv, t_recv, c_send, c_recv, a_send, af_send, a_recv, h_send, h_recv, r_send, r_recv,
):
    qw, tokens = tok.shape
    width = gain.shape[1]
    cr = tokens // CHUNKS
    step_tokens = tokens // STEPS
    half_tokens = tokens // HALVES
    zr = 2 * qw // RING
    f = lax.axis_index("frame")
    h = lax.axis_index("head")
    k, y, c = f // 2, (f % 2) * 2 + h // 2, h % 2
    x, z = k // RING, k % RING
    frames = lax.axis_size("frame")
    frame = 2 * k + c
    home = y // 2
    rel = (y - 2 * c + RING) % RING

    def quarter(yy, cc):
        return (yy % 2) * 2 + cc

    def group_of(yy):
        return (yy % 2) * 2 + yy // 2

    def dev(kk, yy, cc):
        return (kk * 2 + yy // 2, (yy % 2) * 2 + cc)

    q_own = quarter(y, c)
    group = group_of(y)
    yp, ym, yo = (y + 1) % RING, (y + RING - 1) % RING, (y + 2) % RING
    g_m, g_p, g_o = group_of(ym), group_of(yp), group_of(yo)
    other = dev(k, y, 1 - c)
    ks = frames // 2
    far = dev((k + jnp.where(c == 1, 1, ks - 1)) % ks, y, 1 - c)
    target = dev(((frame + 1) % frames) // 2, y, 1 - c)

    barrier = pltpu.get_barrier_semaphore()
    friends = [
        other, far, dev(k, yo, c),
        dev(k, yp, 0), dev(k, yp, 1), dev(k, ym, 0), dev(k, ym, 1),
    ]
    for d in friends:
        pl.semaphore_signal(barrier, inc=1, device_id=d, device_id_type=MESH)

    def along_x(i):
        return dev((x + i) % RING * RING + z, y, 0)

    def along_z(i):
        return dev(x * RING + (z + i) % RING, y, 0)

    @pl.when(c == 0)
    def _():
        for i in range(1, RING):
            for d in (along_x(i), along_z(i)):
                pl.semaphore_signal(barrier, inc=1, device_id=d, device_id_type=MESH)

    pl.semaphore_wait(barrier, len(friends) + 2 * (RING - 1) * (1 - c))

    def span(i, size):
        return pl.ds(i * size if isinstance(i, int) else pl.multiple_of(i * size, size), size)

    def quart(q, size=None):
        return span(q, qw if size is None else size)

    def x_send_to(i, ch, device):
        t = span(ch, cr)
        return rcopy(
            tok.at[:, t], xg.at[quart(q_own), t], x_send.at[i, ch], x_recv.at[q_own, ch], device
        )

    def x_wait(q, ch):
        part = xg.at[quart(q), span(ch, cr)]
        rcopy(part, part, x_send.at[0, 0], x_recv.at[q, ch], other).wait_recv()

    plus = jnp.logical_or(rel == 1, rel == 2)
    off = jnp.where(plus, 0, 1)
    fpair = 2 * (1 - rel % 2)
    fdev = dev(k, jnp.where(plus, yp, ym), c)

    def x_fwd(j, s):
        part = xg.at[quart(fpair + j), span(2 * s + off, cr)]
        return rcopy(part, part, xf_send.at[j, s], x_recv.at[fpair + j, 2 * s + off], fdev)

    def x_local(ch):
        t = span(ch, cr)
        return pltpu.make_async_copy(tok.at[:, t], xg.at[quart(q_own), t], x_recv.at[q_own, ch])

    def x_issue(s):
        a, b = 2 * s, 2 * s + 1
        x_send_to(0, a, dev(k, yp, home)).start()
        x_send_to(1, b, dev(k, ym, home)).start()
        x_send_to(0, b, dev(k, yp, home)).start()
        x_send_to(1, a, dev(k, ym, home)).start()

        @pl.when(c == home)
        def _():
            x_local(a).start()
            x_local(b).start()

        @pl.when(c != home)
        def _():
            x_send_to(2, a, other).start()
            x_send_to(2, b, other).start()

    def w_local(layer):
        return pltpu.make_async_copy(w.at[layer], wbuf.at[layer], w_recv.at[layer])

    def w_give(layer):
        return rcopy(w.at[layer], wbuf.at[layer], w_send.at[layer], w_recv.at[layer], other)

    def w_wait(layer):
        rcopy(wbuf.at[layer], wbuf.at[layer], w_send.at[0], w_recv.at[layer], other).wait_recv()

    def wo1_copies():
        return (
            rcopy(wo.at[1], wo1.at[c], o_send.at[4], o_recv.at[8 + c], other),
            rcopy(bcol.at[1], bo1.at[c], b_send.at[4], b_recv.at[4 + c], other),
        )

    hw = qw // 2

    def wo0_part(i, src, row, size, recv, device):
        return rcopy(src, wo0.at[pl.ds(row, size)], o_send.at[i], o_recv.at[recv], device)

    def bo0_part(i, src, q, device):
        return rcopy(src, bo0.at[quart(q)], b_send.at[i], b_recv.at[q], device)

    def mult(v):
        return pl.multiple_of(v, 32)

    def wo0_own():
        base = q_own * qw
        return (
            wo0_part(0, wo.at[0], mult(base), qw, 2 * q_own, other),
            wo0_part(1, wo.at[0, pl.ds(0, hw)], mult(base), hw, 2 * q_own, dev(k, ym, c)),
            wo0_part(
                2, wo.at[0, pl.ds(hw, hw)], mult(base + hw), hw, 2 * q_own + 1, dev(k, yp, c)
            ),
            bo0_part(0, bcol.at[0], q_own, other),
            bo0_part(1, bcol.at[0], q_own, dev(k, ym, c)),
        )

    q_next = quarter(yp, c)
    q_last = quarter(yp, 1 - c)

    def wo0_fwd():
        return (
            wo0_part(3, wo0.at[quart(q_next)], mult(q_next * qw), qw, 2 * q_next, other),
            bo0_part(2, bo0.at[quart(q_next)], q_next, other),
        )

    def wo0_wait(q, size, recv):
        part = wo0.at[pl.ds(mult(q * qw), size)]
        rcopy(part, part, o_send.at[0], o_recv.at[recv], other).wait_recv()

    def bo0_wait(q):
        bo0_part(0, bo0.at[quart(q)], q, other).wait_recv()

    def ln_qkv(layer, src, s):
        t = span(s, step_tokens)
        wide = step_tokens // 128
        total = 0.0
        for q in range(4):
            total += jnp.sum(src[quart(q), t].astype(f32), 0, keepdims=True)
        mean = total * (1.0 / width)
        total = 0.0
        for q in range(4):
            d = src[quart(q), t].astype(f32) - mean
            total += jnp.sum(d * d, 0, keepdims=True)
        inv = lax.rsqrt(total * (1.0 / width) + 1e-5)
        normed = []
        for q in range(4):
            g = gcol[layer, quart(q), :]
            d = src[quart(q), t].astype(f32) - mean
            normed.append((d * inv * jnp.concatenate([g] * wide, axis=1)).astype(bf16))
        proj = jnp.dot(
            wbuf[layer], jnp.concatenate(normed, axis=0), preferred_element_type=f32
        )
        kv[layer, :, t] = proj[qw:].astype(bf16)
        for p in range(3):
            rows = proj[128 * p : min(128 * (p + 1), qw)] * SCALE
            if p == 2:
                rows = jnp.concatenate([rows, jnp.zeros_like(rows)], axis=0)
            q_s[t, 128 * p : 128 * (p + 1)] = rows.T.astype(bf16)

    def kv_copy(layer, s):
        t = span(s, step_tokens)
        return rcopy(
            kv.at[layer, :, t], kvp.at[layer, :, t],
            kv_send.at[layer, s], kv_recv.at[layer, s], target,
        )

    corner = jnp.logical_and(c == 0, z == 0)
    inner = jnp.logical_and(c == 0, frame > 0)

    def piece(buf, layer, s, i):
        return buf.at[layer, span(i, zr), span(s, half_tokens)]

    def deal(layer, s, i):
        return rcopy(
            piece(kv, layer, s, i), piece(kv0, layer, s, i),
            q_send.at[layer, s, i], q_recv.at[layer, s], along_x(i),
        )

    def lower(layer, s, i, src):
        return rcopy(
            piece(src, layer, s, x), piece(kv0, layer, s, x),
            d_send.at[layer, s, i], q_recv.at[layer, s], along_z(i),
        )

    def spread(layer, s, i, src):
        return rcopy(
            piece(src, layer, s, x), piece(kv0, layer, s, x),
            z_send.at[layer, s, i], z_recv.at[layer, s, x], along_x(i),
        )

    def piece_wait(layer, s, i, recv):
        part = piece(kv0, layer, s, i)
        rcopy(part, part, q_send.at[layer, s, 0], recv, other).wait_recv()

    def root_copy(layer, s):
        t = span(s, half_tokens)
        return pltpu.make_async_copy(
            kv.at[layer, :, t], kv0.at[layer, :, t], t_recv.at[layer, s]
        )

    def core_copy(layer, s):
        part = kv0.at[layer, :, span(s, half_tokens)]
        return rcopy(part, part, c_send.at[layer, s], c_recv.at[layer, s], other)

    def send_kv(layer, s):
        @pl.when(frame < frames - 1)
        def _():
            kv_copy(layer, s).start()

        @pl.when(jnp.logical_and(frame == 0, s % 2 == 1))
        def _():
            p = s // 2
            for i in range(1, RING):
                deal(layer, p, i).start()
            for i in range(1, RING):
                lower(layer, p, i, kv).start()
            for i in range(1, RING):
                spread(layer, p, i, kv).start()
            root_copy(layer, p).start()

        if layer == 1:
            @pl.when(frame == 0)
            def _():
                t = span(s, step_tokens)
                pltpu.make_async_copy(
                    kv.at[layer, :, t], kvp.at[layer, :, t], kv_recv.at[layer, s]
                ).start()

    def down(layer, s):
        @pl.when(jnp.logical_and(corner, x > 0))
        def _():
            piece_wait(layer, s, x, q_recv.at[layer, s])
            for i in range(1, RING):
                lower(layer, s, i, kv0).start()

    def share(layer, s):
        @pl.when(jnp.logical_and(c == 0, z > 0))
        def _():
            piece_wait(layer, s, x, q_recv.at[layer, s])

        @pl.when(inner)
        def _():
            for i in range(1, RING):
                @pl.when(jnp.logical_or(z > 0, x + i != RING))
                def _():
                    spread(layer, s, i, kv0).start()

    def hand_over(layer, s):
        @pl.when(frame == 0)
        def _():
            root_copy(layer, s).wait()

        @pl.when(inner)
        def _():
            for i in range(1, RING):
                j = (x + i) % RING
                piece_wait(layer, s, j, z_recv.at[layer, s, j])

        @pl.when(c == 0)
        def _():
            core_copy(layer, s).start()

    def first_ready(layer):
        @pl.when(c == 1)
        def _():
            for s in range(HALVES):
                core_copy(layer, s).wait_recv()

    def flash(layer, keys, cols, t, size, first):
        count = tokens if cols is None else half_tokens
        cols = slice(None) if cols is None else cols
        lane = lax.broadcasted_iota(jnp.int32, (size, 128), 1)
        found = []
        for head in range(HEADS):
            p = head // 2
            qq = q_s[t, 128 * p : 128 * (p + 1)]
            if head < 4:
                qq = jnp.where((lane // 64) == head % 2, qq, jnp.zeros_like(qq))
                kk = keys[layer, 128 * p : 128 * (p + 1), cols]
                values = [keys[layer, qw + 128 * p : qw + 128 * (p + 1), cols]]
            else:
                qq = qq[:, :64]
                kk = keys[layer, 256:qw, cols]
                values = [keys[layer, qw + 256 : 2 * qw, cols], jnp.zeros((64, count), bf16)]
            values = jnp.concatenate(values + [jnp.ones((128, count), bf16)], axis=0)
            scores = jnp.dot(qq, kk, preferred_element_type=f32)
            top = jnp.max(scores, -1, keepdims=True)
            wide = top
            if not first:
                before = m_s[head, t, :]
                top = jnp.maximum(before, top)
                wide = jnp.concatenate([top] * (count // 128), axis=1)
            e = jnp.exp2(scores - wide).astype(bf16)
            o = lax.dot_general(e, values, (((1,), (1,)), ((), ())), preferred_element_type=f32)
            acc, total = o[:, :128], o[:, 128:]
            if not first:
                alpha = jnp.exp2(before - top)
                acc = acc_s[head, t, :] * alpha + acc
                total = l_s[head, t, :] * alpha + total
            found.append((acc, total, jnp.broadcast_to(top, (size, 128))))
        return found, lane

    def update(layer, keys, cols, first):
        def body(s, carry):
            t = span(s, half_tokens)
            found, _ = flash(layer, keys, cols, t, half_tokens, first)
            for head, (acc, total, top) in enumerate(found):
                acc_s[head, t, :] = acc
                l_s[head, t, :] = total
                m_s[head, t, :] = top
            return carry

        lax.fori_loop(0, HALVES, body, 0)

    def finish(layer, keys, cols, s, dst):
        t = span(s, step_tokens)
        found, lane = flash(layer, keys, cols, t, step_tokens, False)
        pieces = [acc / total for acc, total, _ in found]
        base = group * qw
        dst[pl.ds(mult(base), 128), t] = jnp.where(lane < 64, pieces[0], pieces[1]).T.astype(bf16)
        dst[pl.ds(mult(base + 128), 128), t] = (
            jnp.where(lane < 64, pieces[2], pieces[3]).T.astype(bf16)
        )
        dst[pl.ds(mult(base + 256), 64), t] = pieces[4].T[:64].astype(bf16)

    def half_cols(part):
        return slice(part * half_tokens, (part + 1) * half_tokens)

    def wait_previous(layer, part):
        for s in range(2 * part, 2 * part + 2):
            kv_copy(layer, s).wait_recv()

    def a_copy(direction, ch):
        part = attg.at[quart(group), span(ch, cr)]
        return rcopy(
            part, part, a_send.at[direction, ch], a_recv.at[group, ch],
            dev(k, yp if direction == 0 else ym, c),
        )

    def a_fwd(direction, s):
        ch = 2 * s + direction
        g = g_m if direction == 0 else g_p
        part = attg.at[quart(g), span(ch, cr)]
        return rcopy(
            part, part, af_send.at[direction, s], a_recv.at[g, ch],
            dev(k, yp if direction == 0 else ym, c),
        )

    def a_wait(g, ch):
        part = attg.at[quart(g), span(ch, cr)]
        rcopy(part, part, a_send.at[0, 0], a_recv.at[g, ch], other).wait_recv()

    def a_forward(s):
        a_wait(g_m, 2 * s)
        a_fwd(0, s).start()
        a_wait(g_p, 2 * s + 1)
        a_fwd(1, s).start()

    at_home = rel < 2
    mate = dev(k, jnp.where(rel == 0, yp, ym), c)
    near = dev(k, jnp.where(rel == 2, ym, yp), c)
    across = dev(k, yo, c)

    def h_copy(i, s, device):
        part = att1.at[quart(group), span(s, step_tokens)]
        return rcopy(part, part, h_send.at[i, s], h_recv.at[group, s], device)

    def h_wait(g, s):
        part = att1.at[quart(g), span(s, step_tokens)]
        rcopy(part, part, h_send.at[0, 0], h_recv.at[g, s], other).wait_recv()

    def r_copy(s):
        t = span(s, step_tokens)
        return rcopy(res.at[1 - c, :, t], out.at[:, t], r_send.at[s], r_recv.at[s], other)

    x_issue(0)
    x_issue(1)

    @pl.when(c == home)
    def _():
        w_local(0).start()
        w_give(0).start()

    def column(row):
        return jnp.broadcast_to(row, (128, row.shape[1])).T

    for layer in range(BLOCKS):
        gcol[layer] = column(gain[layer : layer + 1, :])
        row = bias[layer : layer + 1, :].astype(f32)
        row = jnp.concatenate([row, jnp.zeros((1, 384 - qw), f32)], axis=1)
        bcol[layer] = column(row)[:qw]

    def first(s, carry):
        x_wait(fpair, 2 * s + off)
        x_wait(fpair + 1, 2 * s + off)
        x_fwd(0, s).start()
        x_fwd(1, s).start()

        @pl.when(s < STEPS - 2)
        def _():
            x_issue(s + 2)

        @pl.when(s == 2)
        def _():
            down(0, 0)

        @pl.when(s == 3)
        def _():
            share(0, 0)

        x_wait(fpair, 2 * s + 1 - off)
        x_wait(fpair + 1, 2 * s + 1 - off)
        for j in range(2):
            x_wait(2 - fpair + j, 2 * s)
            x_wait(2 - fpair + j, 2 * s + 1)

        @pl.when(s == 0)
        def _():
            w_wait(0)

        ln_qkv(0, xg, s)
        send_kv(0, s)

        return carry

    lax.fori_loop(0, STEPS, first, 0)

    @pl.when(c == home)
    def _():
        w_local(1).start()
        w_give(1).start()
        pltpu.make_async_copy(wo.at[1], wo1.at[c], o_recv.at[8 + c]).start()
        pltpu.make_async_copy(bcol.at[1], bo1.at[c], b_recv.at[4 + c]).start()

    @pl.when(c != home)
    def _():
        for cp in wo1_copies():
            cp.start()

    pltpu.make_async_copy(wo.at[0], wo0.at[quart(q_own)], o_recv.at[2 * q_own]).start()
    pltpu.make_async_copy(bcol.at[0], bo0.at[quart(q_own)], b_recv.at[q_own]).start()
    for cp in wo0_own():
        cp.start()

    down(0, 1)

    @pl.when(frame > 0)
    def _():
        wait_previous(0, 0)
        update(0, kvp, half_cols(0), True)

    @pl.when(frame == 0)
    def _():
        acc_s[...] = jnp.zeros(acc_s.shape, f32)
        l_s[...] = jnp.zeros(l_s.shape, f32)
        m_s[...] = jnp.full(m_s.shape, -jnp.inf, f32)

    share(0, 1)
    hand_over(0, 0)

    @pl.when(frame > 0)
    def _():
        wait_previous(0, 1)
        update(0, kvp, half_cols(1), False)

    hand_over(0, 1)
    first_ready(0)

    def second0(s, carry):
        finish(0, kv0, None, s, attg)
        a_copy(0, 2 * s).start()
        a_copy(1, 2 * s + 1).start()
        a_copy(0, 2 * s + 1).start()
        a_copy(1, 2 * s).start()

        @pl.when(s == 0)
        def _():
            wo0_wait(q_next, hw, 2 * q_next)
            wo0_wait(q_next, hw, 2 * q_next + 1)
            bo0_wait(q_next)
            for cp in wo0_fwd():
                cp.start()

        @pl.when(s >= 2)
        def _():
            a_forward(s - 2)

        return carry

    lax.fori_loop(0, STEPS, second0, 0)
    for q in (q_own, quarter(y, 1 - c), q_last):
        wo0_wait(q, qw, 2 * q)
        bo0_wait(q)
    w_wait(1)

    def third(s, carry):
        @pl.when(s < STEPS - 2)
        def _():
            a_forward(s + 2)

        a_wait(g_m, 2 * s + 1)
        a_wait(g_p, 2 * s)
        a_wait(g_o, 2 * s)
        a_wait(g_o, 2 * s + 1)
        t = span(s, step_tokens)
        for q in range(4):
            summed = jnp.dot(wo0[quart(q), :], attg[:, t], preferred_element_type=f32)
            b = jnp.concatenate([bo0[quart(q), :]] * (step_tokens // 128), axis=1)
            x1[quart(q), t] = (summed + b + xg[quart(q), t].astype(f32)).astype(bf16)
        ln_qkv(1, x1, s)
        send_kv(1, s)

        @pl.when(s == 0)
        def _():
            down(1, 0)

        @pl.when(s == 1)
        def _():
            share(1, 0)
            down(1, 1)

        @pl.when(s == 2)
        def _():
            share(1, 1)
            hand_over(1, 0)

        return carry

    lax.fori_loop(0, STEPS, third, 0)

    hand_over(1, 1)
    wait_previous(1, 0)
    update(1, kvp, half_cols(0), True)
    first_ready(1)
    update(1, kv0, None, False)
    wait_previous(1, 1)

    def second1(s, carry):
        finish(1, kvp, half_cols(1), s, att1)

        @pl.when(at_home)
        def _():
            h_copy(0, s, mate).start()

        @pl.when(jnp.logical_not(at_home))
        def _():
            h_copy(0, s, near).start()
            h_copy(1, s, across).start()

        return carry

    lax.fori_loop(0, STEPS, second1, 0)

    @pl.when(at_home)
    def _():
        for j in range(2):
            rcopy(wo.at[1], wo1.at[j], o_send.at[0], o_recv.at[8 + j], other).wait_recv()
            rcopy(bcol.at[1], bo1.at[j], b_send.at[0], b_recv.at[4 + j], other).wait_recv()

        def last(s, carry):
            t = span(s, step_tokens)
            for g in (g_m, g_p, g_o):
                h_wait(g, s)
            for j in range(2):
                summed = jnp.dot(wo1[j], att1[:, t], preferred_element_type=f32)
                b = jnp.concatenate([bo1[j]] * (step_tokens // 128), axis=1)
                before = x1[quart((y % 2) * 2 + j), t].astype(f32)
                res[j, :, t] = (summed + b + before).astype(bf16)
            r_copy(s).start()
            out[:, t] = res[c, :, t]
            return carry

        lax.fori_loop(0, STEPS, last, 0)
        for s in range(STEPS):
            r_copy(s).wait_send()
            h_copy(0, s, mate).wait_send()

    @pl.when(jnp.logical_not(at_home))
    def _():
        for s in range(STEPS):
            h_copy(0, s, near).wait_send()
            h_copy(1, s, across).wait_send()
            r_copy(s).wait_recv()

    for s in range(STEPS):
        for j in range(2):
            x_fwd(j, s).wait_send()
            a_fwd(j, s).wait_send()
    for ch in range(CHUNKS):
        x_send_to(0, ch, other).wait_send()
        x_send_to(1, ch, other).wait_send()
        a_copy(0, ch).wait_send()
        a_copy(1, ch).wait_send()
    for cp in wo0_own() + wo0_fwd():
        cp.wait_send()

    @pl.when(c == home)
    def _():
        for layer in range(BLOCKS):
            w_give(layer).wait_send()

    @pl.when(c != home)
    def _():
        for cp in wo1_copies():
            cp.wait_send()
        for ch in range(CHUNKS):
            x_send_to(2, ch, other).wait_send()

    for layer in range(BLOCKS):
        @pl.when(frame < frames - 1)
        def _():
            for s in range(STEPS):
                kv_copy(layer, s).wait_send()

        for s in range(HALVES):
            @pl.when(corner)
            def _():
                for i in range(1, RING):
                    lower(layer, s, i, kv0).wait_send()

            @pl.when(c == 0)
            def _():
                core_copy(layer, s).wait_send()
                for i in range(1, RING):
                    @pl.when(jnp.logical_or(k == 0, jnp.logical_or(z > 0, x + i != RING)))
                    def _():
                        spread(layer, s, i, kv0).wait_send()

            @pl.when(frame == 0)
            def _():
                for i in range(1, RING):
                    deal(layer, s, i).wait_send()


def shards(tokens, norm_gain, w_qkv, w_out, out_bias):
    rows, qw = tokens.shape[1:]
    width = w_qkv.shape[1]
    w = jnp.transpose(w_qkv, (0, 2, 3, 1)).reshape(BLOCKS, 3 * qw, width)
    wo = jnp.swapaxes(w_out, 1, 2)
    any_spec = pl.BlockSpec(memory_space=pl.ANY)
    vmem = pl.BlockSpec(memory_space=pltpu.VMEM)
    dma = pltpu.SemaphoreType.DMA
    result = pl.pallas_call(
        kernel,
        out_shape=jax.ShapeDtypeStruct((qw, rows), bf16),
        in_specs=[any_spec, vmem, any_spec, any_spec, vmem],
        out_specs=vmem,
        scratch_shapes=[
            pltpu.VMEM((width, rows), bf16),
            pltpu.VMEM((width, rows), bf16),
            pltpu.VMEM((BLOCKS, 3 * qw, width), bf16),
            pltpu.VMEM((width, width), bf16),
            pltpu.VMEM((width, 128), f32),
            pltpu.VMEM((2, qw, width), bf16),
            pltpu.VMEM((2, qw, 128), f32),
            pltpu.VMEM((rows, 384), bf16),
            pltpu.VMEM((BLOCKS, 2 * qw, rows), bf16),
            pltpu.VMEM((BLOCKS, 2 * qw, rows), bf16),
            pltpu.VMEM((BLOCKS, 2 * qw, rows), bf16),
            pltpu.VMEM((width, rows), bf16),
            pltpu.VMEM((width, rows), bf16),
            pltpu.VMEM((2, qw, rows), bf16),
            pltpu.VMEM((HEADS, rows, 128), f32),
            pltpu.VMEM((HEADS, rows, 128), f32),
            pltpu.VMEM((HEADS, rows, 128), f32),
            pltpu.VMEM((BLOCKS, width, 128), f32),
            pltpu.VMEM((BLOCKS, qw, 128), f32),
            dma((3, CHUNKS)), dma((2, STEPS)), dma((4, CHUNKS)), dma((2,)), dma((2,)),
            dma((5,)), dma((10,)), dma((5,)), dma((6,)),
            dma((BLOCKS, STEPS)), dma((BLOCKS, STEPS)),
            dma((BLOCKS, HALVES, 4)), dma((BLOCKS, HALVES)), dma((BLOCKS, HALVES, 4)),
            dma((BLOCKS, HALVES, 4)), dma((BLOCKS, HALVES, 4)),
            dma((BLOCKS, HALVES)), dma((BLOCKS, HALVES)), dma((BLOCKS, HALVES)),
            dma((2, CHUNKS)), dma((2, STEPS)), dma((4, CHUNKS)),
            dma((2, STEPS)), dma((4, STEPS)), dma((STEPS,)), dma((STEPS,)),
        ],
        compiler_params=pltpu.CompilerParams(
            collective_id=0, has_side_effects=True, vmem_limit_bytes=60 << 20
        ),
        name="video_blocks",
    )(jnp.swapaxes(tokens[0], 0, 1), norm_gain, w, wo, out_bias)
    return jnp.swapaxes(result, 0, 1)[None]


def solution(mesh):
    placed = (
        P("frame", None, "head"),
        P(),
        P(None, None, None, "head"),
        P(None, None, "head"),
        P(None, "head"),
    )
    return jax.shard_map(
        shards, mesh=mesh, in_specs=placed, out_specs=P("frame", None, "head"), check_vma=False
    )
```

```python
import functools

import jax
import jax.numpy as jnp
from jax import lax
from jax.experimental import pallas as pl
from jax.experimental.pallas import tpu as pltpu
from jax.sharding import PartitionSpec as P

HEAD_DIM = 64
BLOCKS = 2
HEADS = 5
CHUNKS = 8
STEPS = 4
HALVES = 2
RING = 4
MESH = pl.DeviceIdType.MESH
f32 = jnp.float32
bf16 = jnp.bfloat16
SCALE = HEAD_DIM**-0.5 * 1.4426950408889634


def rcopy(src, dst, send, recv, device):
    return pltpu.make_async_remote_copy(
        src_ref=src,
        dst_ref=dst,
        send_sem=send,
        recv_sem=recv,
        device_id=device,
        device_id_type=MESH,
    )


def kernel(
    tok, gain, w, wo, bias, out,
    xg, x1, wbuf, wo0, bo0, wo1, bo1, q_s, kv, kvp, kv0, attg, att1, res, acc_s, m_s, l_s, gcol, bcol,
    x_send, xf_send, x_recv, w_send, w_recv, o_send, o_recv, b_send, b_recv,
    kv_send, kv_recv, q_send, q_recv, d_send, z_send, z_recv, t_recv, c_send, c_recv, a_send, af_send, a_recv, h_send, h_recv, r_send, r_recv,
):
    qw, tokens = tok.shape
    width = gain.shape[1]
    cr = tokens // CHUNKS
    step_tokens = tokens // STEPS
    half_tokens = tokens // HALVES
    zr = 2 * qw // RING
    f = lax.axis_index("frame")
    h = lax.axis_index("head")
    k, y, c = f // 2, (f % 2) * 2 + h // 2, h % 2
    x, z = k // RING, k % RING
    frames = lax.axis_size("frame")
    frame = 2 * k + c
    home = y // 2
    rel = (y - 2 * c + RING) % RING

    def quarter(yy, cc):
        return (yy % 2) * 2 + cc

    def group_of(yy):
        return (yy % 2) * 2 + yy // 2

    def dev(kk, yy, cc):
        return (kk * 2 + yy // 2, (yy % 2) * 2 + cc)

    q_own = quarter(y, c)
    group = group_of(y)
    yp, ym, yo = (y + 1) % RING, (y + RING - 1) % RING, (y + 2) % RING
    g_m, g_p, g_o = group_of(ym), group_of(yp), group_of(yo)
    other = dev(k, y, 1 - c)
    ks = frames // 2
    far = dev((k + jnp.where(c == 1, 1, ks - 1)) % ks, y, 1 - c)
    target = dev(((frame + 1) % frames) // 2, y, 1 - c)

    barrier = pltpu.get_barrier_semaphore()
    friends = [
        other, far, dev(k, yo, c),
        dev(k, yp, 0), dev(k, yp, 1), dev(k, ym, 0), dev(k, ym, 1),
    ]
    for d in friends:
        pl.semaphore_signal(barrier, inc=1, device_id=d, device_id_type=MESH)

    def along_x(i):
        return dev((x + i) % RING * RING + z, y, 0)

    def along_z(i):
        return dev(x * RING + (z + i) % RING, y, 0)

    @pl.when(c == 0)
    def _():
        for i in range(1, RING):
            for d in (along_x(i), along_z(i)):
                pl.semaphore_signal(barrier, inc=1, device_id=d, device_id_type=MESH)

    pl.semaphore_wait(barrier, len(friends) + 2 * (RING - 1) * (1 - c))

    def span(i, size):
        return pl.ds(i * size if isinstance(i, int) else pl.multiple_of(i * size, size), size)

    def quart(q, size=None):
        return span(q, qw if size is None else size)

    def x_send_to(i, ch, device):
        t = span(ch, cr)
        return rcopy(
            tok.at[:, t], xg.at[quart(q_own), t], x_send.at[i, ch], x_recv.at[q_own, ch], device
        )

    def x_wait(q, ch):
        part = xg.at[quart(q), span(ch, cr)]
        rcopy(part, part, x_send.at[0, 0], x_recv.at[q, ch], other).wait_recv()

    plus = jnp.logical_or(rel == 1, rel == 2)
    off = jnp.where(plus, 0, 1)
    fpair = 2 * (1 - rel % 2)
    fdev = dev(k, jnp.where(plus, yp, ym), c)

    def x_fwd(j, s):
        part = xg.at[quart(fpair + j), span(2 * s + off, cr)]
        return rcopy(part, part, xf_send.at[j, s], x_recv.at[fpair + j, 2 * s + off], fdev)

    def x_local(ch):
        t = span(ch, cr)
        return pltpu.make_async_copy(tok.at[:, t], xg.at[quart(q_own), t], x_recv.at[q_own, ch])

    def x_issue(s):
        a, b = 2 * s, 2 * s + 1
        x_send_to(0, a, dev(k, yp, home)).start()
        x_send_to(1, b, dev(k, ym, home)).start()
        x_send_to(0, b, dev(k, yp, home)).start()
        x_send_to(1, a, dev(k, ym, home)).start()

        @pl.when(c == home)
        def _():
            x_local(a).start()
            x_local(b).start()

        @pl.when(c != home)
        def _():
            x_send_to(2, a, other).start()
            x_send_to(2, b, other).start()

    def w_local(layer):
        return pltpu.make_async_copy(w.at[layer], wbuf.at[layer], w_recv.at[layer])

    def w_give(layer):
        return rcopy(w.at[layer], wbuf.at[layer], w_send.at[layer], w_recv.at[layer], other)

    def w_wait(layer):
        rcopy(wbuf.at[layer], wbuf.at[layer], w_send.at[0], w_recv.at[layer], other).wait_recv()

    def wo1_copies():
        return (
            rcopy(wo.at[1], wo1.at[c], o_send.at[4], o_recv.at[8 + c], other),
            rcopy(bcol.at[1], bo1.at[c], b_send.at[4], b_recv.at[4 + c], other),
        )

    hw = qw // 2

    def wo0_part(i, src, row, size, recv, device):
        return rcopy(src, wo0.at[pl.ds(row, size)], o_send.at[i], o_recv.at[recv], device)

    def bo0_part(i, src, q, device):
        return rcopy(src, bo0.at[quart(q)], b_send.at[i], b_recv.at[q], device)

    def mult(v):
        return pl.multiple_of(v, 32)

    def wo0_own():
        base = q_own * qw
        return (
            wo0_part(0, wo.at[0], mult(base), qw, 2 * q_own, other),
            wo0_part(1, wo.at[0, pl.ds(0, hw)], mult(base), hw, 2 * q_own, dev(k, ym, c)),
            wo0_part(
                2, wo.at[0, pl.ds(hw, hw)], mult(base + hw), hw, 2 * q_own + 1, dev(k, yp, c)
            ),
            bo0_part(0, bcol.at[0], q_own, other),
            bo0_part(1, bcol.at[0], q_own, dev(k, ym, c)),
        )

    q_next = quarter(yp, c)
    q_last = quarter(yp, 1 - c)

    def wo0_fwd():
        return (
            wo0_part(3, wo0.at[quart(q_next)], mult(q_next * qw), qw, 2 * q_next, other),
            bo0_part(2, bo0.at[quart(q_next)], q_next, other),
        )

    def wo0_wait(q, size, recv):
        part = wo0.at[pl.ds(mult(q * qw), size)]
        rcopy(part, part, o_send.at[0], o_recv.at[recv], other).wait_recv()

    def bo0_wait(q):
        bo0_part(0, bo0.at[quart(q)], q, other).wait_recv()

    def ln_qkv(layer, src, s):
        t = span(s, step_tokens)
        wide = step_tokens // 128
        total = 0.0
        for q in range(4):
            total += jnp.sum(src[quart(q), t].astype(f32), 0, keepdims=True)
        mean = total * (1.0 / width)
        total = 0.0
        for q in range(4):
            d = src[quart(q), t].astype(f32) - mean
            total += jnp.sum(d * d, 0, keepdims=True)
        inv = lax.rsqrt(total * (1.0 / width) + 1e-5)
        normed = []
        for q in range(4):
            g = gcol[layer, quart(q), :]
            d = src[quart(q), t].astype(f32) - mean
            normed.append((d * inv * jnp.concatenate([g] * wide, axis=1)).astype(bf16))
        proj = jnp.dot(
            wbuf[layer], jnp.concatenate(normed, axis=0), preferred_element_type=f32
        )
        kv[layer, :, t] = proj[qw:].astype(bf16)
        for p in range(3):
            rows = proj[128 * p : min(128 * (p + 1), qw)] * SCALE
            if p == 2:
                rows = jnp.concatenate([rows, jnp.zeros_like(rows)], axis=0)
            q_s[t, 128 * p : 128 * (p + 1)] = rows.T.astype(bf16)

    def kv_copy(layer, s):
        t = span(s, step_tokens)
        return rcopy(
            kv.at[layer, :, t], kvp.at[layer, :, t],
            kv_send.at[layer, s], kv_recv.at[layer, s], target,
        )

    corner = jnp.logical_and(c == 0, z == 0)
    inner = jnp.logical_and(c == 0, frame > 0)

    def piece(buf, layer, s, i):
        return buf.at[layer, span(i, zr), span(s, step_tokens)]

    def deal(layer, s, i):
        return rcopy(
            piece(kv, layer, s, i), piece(kv0, layer, s, i),
            q_send.at[layer, s, i], q_recv.at[layer, s], along_x(i),
        )

    def lower(layer, s, i, src):
        return rcopy(
            piece(src, layer, s, x), piece(kv0, layer, s, x),
            d_send.at[layer, s, i], q_recv.at[layer, s], along_z(i),
        )

    def spread(layer, s, i, src):
        return rcopy(
            piece(src, layer, s, x), piece(kv0, layer, s, x),
            z_send.at[layer, s, i], z_recv.at[layer, s, x], along_x(i),
        )

    def piece_wait(layer, s, i, recv):
        part = piece(kv0, layer, s, i)
        rcopy(part, part, q_send.at[layer, s, 0], recv, other).wait_recv()

    def root_copy(layer, s):
        t = span(s, step_tokens)
        return pltpu.make_async_copy(
            kv.at[layer, :, t], kv0.at[layer, :, t], t_recv.at[layer, s]
        )

    def core_copy(layer, s):
        part = kv0.at[layer, :, span(s, step_tokens)]
        return rcopy(part, part, c_send.at[layer, s], c_recv.at[layer, s], other)

    def send_kv(layer, s):
        @pl.when(frame < frames - 1)
        def _():
            kv_copy(layer, s).start()

        @pl.when(frame == 0)
        def _():
            for i in range(1, RING):
                deal(layer, s, i).start()
            for i in range(1, RING):
                lower(layer, s, i, kv).start()
            for i in range(1, RING):
                spread(layer, s, i, kv).start()
            root_copy(layer, s).start()

        if layer == 1:
            @pl.when(frame == 0)
            def _():
                t = span(s, step_tokens)
                pltpu.make_async_copy(
                    kv.at[layer, :, t], kvp.at[layer, :, t], kv_recv.at[layer, s]
                ).start()

    def down(layer, s):
        @pl.when(jnp.logical_and(corner, x > 0))
        def _():
            piece_wait(layer, s, x, q_recv.at[layer, s])
            for i in range(1, RING):
                lower(layer, s, i, kv0).start()

    def share(layer, s):
        @pl.when(jnp.logical_and(c == 0, z > 0))
        def _():
            piece_wait(layer, s, x, q_recv.at[layer, s])

        @pl.when(inner)
        def _():
            for i in range(1, RING):
                @pl.when(jnp.logical_or(z > 0, x + i != RING))
                def _():
                    spread(layer, s, i, kv0).start()

    def hand_over(layer, s):
        @pl.when(frame == 0)
        def _():
            root_copy(layer, s).wait()

        @pl.when(inner)
        def _():
            for i in range(1, RING):
                j = (x + i) % RING
                piece_wait(layer, s, j, z_recv.at[layer, s, j])

        @pl.when(c == 0)
        def _():
            core_copy(layer, s).start()

    def first_ready(layer):
        @pl.when(c == 1)
        def _():
            for s in range(STEPS):
                core_copy(layer, s).wait_recv()

    def flash(layer, keys, cols, t, size, first):
        count = tokens if cols is None else half_tokens
        cols = slice(None) if cols is None else cols
        lane = lax.broadcasted_iota(jnp.int32, (size, 128), 1)
        found = []
        for head in range(HEADS):
            p = head // 2
            qq = q_s[t, 128 * p : 128 * (p + 1)]
            if head < 4:
                qq = jnp.where((lane // 64) == head % 2, qq, jnp.zeros_like(qq))
                kk = keys[layer, 128 * p : 128 * (p + 1), cols]
                values = [keys[layer, qw + 128 * p : qw + 128 * (p + 1), cols]]
            else:
                qq = qq[:, :64]
                kk = keys[layer, 256:qw, cols]
                values = [keys[layer, qw + 256 : 2 * qw, cols], jnp.zeros((64, count), bf16)]
            values = jnp.concatenate(values + [jnp.ones((128, count), bf16)], axis=0)
            scores = jnp.dot(qq, kk, preferred_element_type=f32)
            top = jnp.max(scores, -1, keepdims=True)
            wide = top
            if not first:
                before = m_s[head, t, :]
                top = jnp.maximum(before, top)
                wide = jnp.concatenate([top] * (count // 128), axis=1)
            e = jnp.exp2(scores - wide).astype(bf16)
            o = lax.dot_general(e, values, (((1,), (1,)), ((), ())), preferred_element_type=f32)
            acc, total = o[:, :128], o[:, 128:]
            if not first:
                alpha = jnp.exp2(before - top)
                acc = acc_s[head, t, :] * alpha + acc
                total = l_s[head, t, :] * alpha + total
            found.append((acc, total, jnp.broadcast_to(top, (size, 128))))
        return found, lane

    def update(layer, keys, cols, first, between=None):
        size = half_tokens if between is not None else tokens

        def body(s, carry):
            t = span(s, size)
            found, _ = flash(layer, keys, cols, t, size, first)
            for head, (acc, total, top) in enumerate(found):
                acc_s[head, t, :] = acc
                l_s[head, t, :] = total
                m_s[head, t, :] = top
            if between is not None:
                pl.when(s == 0)(between)
            return carry

        lax.fori_loop(0, tokens // size, body, 0)

    def finish(layer, keys, cols, s, dst):
        t = span(s, step_tokens)
        found, lane = flash(layer, keys, cols, t, step_tokens, False)
        pieces = [acc / total for acc, total, _ in found]
        base = group * qw
        dst[pl.ds(mult(base), 128), t] = jnp.where(lane < 64, pieces[0], pieces[1]).T.astype(bf16)
        dst[pl.ds(mult(base + 128), 128), t] = (
            jnp.where(lane < 64, pieces[2], pieces[3]).T.astype(bf16)
        )
        dst[pl.ds(mult(base + 256), 64), t] = pieces[4].T[:64].astype(bf16)

    def half_cols(part):
        return slice(part * half_tokens, (part + 1) * half_tokens)

    def wait_previous(layer, part):
        for s in range(2 * part, 2 * part + 2):
            kv_copy(layer, s).wait_recv()

    def a_copy(direction, ch):
        part = attg.at[quart(group), span(ch, cr)]
        return rcopy(
            part, part, a_send.at[direction, ch], a_recv.at[group, ch],
            dev(k, yp if direction == 0 else ym, c),
        )

    def a_fwd(direction, s):
        ch = 2 * s + direction
        g = g_m if direction == 0 else g_p
        part = attg.at[quart(g), span(ch, cr)]
        return rcopy(
            part, part, af_send.at[direction, s], a_recv.at[g, ch],
            dev(k, yp if direction == 0 else ym, c),
        )

    def a_wait(g, ch):
        part = attg.at[quart(g), span(ch, cr)]
        rcopy(part, part, a_send.at[0, 0], a_recv.at[g, ch], other).wait_recv()

    def a_forward(s):
        a_wait(g_m, 2 * s)
        a_fwd(0, s).start()
        a_wait(g_p, 2 * s + 1)
        a_fwd(1, s).start()

    at_home = rel < 2
    mate = dev(k, jnp.where(rel == 0, yp, ym), c)
    near = dev(k, jnp.where(rel == 2, ym, yp), c)
    across = dev(k, yo, c)

    def h_copy(i, s, device):
        part = att1.at[quart(group), span(s, step_tokens)]
        return rcopy(part, part, h_send.at[i, s], h_recv.at[group, s], device)

    def h_wait(g, s):
        part = att1.at[quart(g), span(s, step_tokens)]
        rcopy(part, part, h_send.at[0, 0], h_recv.at[g, s], other).wait_recv()

    def r_copy(s):
        t = span(s, step_tokens)
        return rcopy(res.at[1 - c, :, t], out.at[:, t], r_send.at[s], r_recv.at[s], other)

    x_issue(0)
    x_issue(1)

    @pl.when(c == home)
    def _():
        w_local(0).start()
        w_give(0).start()

    def column(row):
        return jnp.broadcast_to(row, (128, row.shape[1])).T

    for layer in range(BLOCKS):
        gcol[layer] = column(gain[layer : layer + 1, :])
        row = bias[layer : layer + 1, :].astype(f32)
        row = jnp.concatenate([row, jnp.zeros((1, 384 - qw), f32)], axis=1)
        bcol[layer] = column(row)[:qw]

    def first(s, carry):
        x_wait(fpair, 2 * s + off)
        x_wait(fpair + 1, 2 * s + off)
        x_fwd(0, s).start()
        x_fwd(1, s).start()

        @pl.when(s < STEPS - 2)
        def _():
            x_issue(s + 2)

        @pl.when(s > 0)
        def _():
            down(0, s - 1)

        @pl.when(s > 1)
        def _():
            share(0, s - 2)

        @pl.when(s == 3)
        def _():
            pltpu.make_async_copy(wo.at[0], wo0.at[quart(q_own)], o_recv.at[2 * q_own]).start()
            pltpu.make_async_copy(bcol.at[0], bo0.at[quart(q_own)], b_recv.at[q_own]).start()
            for cp in wo0_own():
                cp.start()

        x_wait(fpair, 2 * s + 1 - off)
        x_wait(fpair + 1, 2 * s + 1 - off)
        for j in range(2):
            x_wait(2 - fpair + j, 2 * s)
            x_wait(2 - fpair + j, 2 * s + 1)

        @pl.when(s == 0)
        def _():
            w_wait(0)

        ln_qkv(0, xg, s)
        send_kv(0, s)

        return carry

    lax.fori_loop(0, STEPS, first, 0)

    @pl.when(c == home)
    def _():
        w_local(1).start()
        w_give(1).start()
        pltpu.make_async_copy(wo.at[1], wo1.at[c], o_recv.at[8 + c]).start()
        pltpu.make_async_copy(bcol.at[1], bo1.at[c], b_recv.at[4 + c]).start()

    @pl.when(c != home)
    def _():
        for cp in wo1_copies():
            cp.start()

    def pass_on():
        wo0_wait(q_next, hw, 2 * q_next)
        wo0_wait(q_next, hw, 2 * q_next + 1)
        bo0_wait(q_next)
        for cp in wo0_fwd():
            cp.start()

    share(0, 2)

    @pl.when(frame > 0)
    def _():
        wait_previous(0, 0)
        update(0, kvp, half_cols(0), True, lambda: down(0, 3))
        pass_on()

    @pl.when(frame == 0)
    def _():
        acc_s[...] = jnp.zeros(acc_s.shape, f32)
        l_s[...] = jnp.zeros(l_s.shape, f32)
        m_s[...] = jnp.full(m_s.shape, -jnp.inf, f32)

    share(0, 3)

    @pl.when(frame > 0)
    def _():
        wait_previous(0, 1)
        update(0, kvp, half_cols(1), False)

    for s in range(STEPS):
        hand_over(0, s)
    first_ready(0)

    def second0(s, carry):
        finish(0, kv0, None, s, attg)
        a_copy(0, 2 * s).start()
        a_copy(1, 2 * s + 1).start()
        a_copy(0, 2 * s + 1).start()
        a_copy(1, 2 * s).start()

        @pl.when(jnp.logical_and(frame == 0, s == 1))
        def _():
            pass_on()

        @pl.when(s >= 2)
        def _():
            a_forward(s - 2)

        return carry

    lax.fori_loop(0, STEPS, second0, 0)
    for q in (q_own, quarter(y, 1 - c), q_last):
        wo0_wait(q, qw, 2 * q)
        bo0_wait(q)
    w_wait(1)

    def third(s, carry):
        @pl.when(s < STEPS - 2)
        def _():
            a_forward(s + 2)

        a_wait(g_m, 2 * s + 1)
        a_wait(g_p, 2 * s)
        a_wait(g_o, 2 * s)
        a_wait(g_o, 2 * s + 1)
        t = span(s, step_tokens)
        for q in range(4):
            summed = jnp.dot(wo0[quart(q), :], attg[:, t], preferred_element_type=f32)
            b = jnp.concatenate([bo0[quart(q), :]] * (step_tokens // 128), axis=1)
            x1[quart(q), t] = (summed + b + xg[quart(q), t].astype(f32)).astype(bf16)
        ln_qkv(1, x1, s)
        send_kv(1, s)

        down(1, s)

        @pl.when(s > 0)
        def _():
            share(1, s - 1)

        return carry

    lax.fori_loop(0, STEPS, third, 0)

    share(1, 3)
    wait_previous(1, 0)
    update(1, kvp, half_cols(0), True)
    for s in range(STEPS):
        hand_over(1, s)
    first_ready(1)
    update(1, kv0, None, False)
    wait_previous(1, 1)

    def second1(s, carry):
        finish(1, kvp, half_cols(1), s, att1)

        @pl.when(at_home)
        def _():
            h_copy(0, s, mate).start()

        @pl.when(jnp.logical_not(at_home))
        def _():
            h_copy(0, s, near).start()
            h_copy(1, s, across).start()

        return carry

    lax.fori_loop(0, STEPS, second1, 0)

    @pl.when(at_home)
    def _():
        for j in range(2):
            rcopy(wo.at[1], wo1.at[j], o_send.at[0], o_recv.at[8 + j], other).wait_recv()
            rcopy(bcol.at[1], bo1.at[j], b_send.at[0], b_recv.at[4 + j], other).wait_recv()

        def last(s, carry):
            t = span(s, step_tokens)
            for g in (g_m, g_p, g_o):
                h_wait(g, s)
            for j in range(2):
                summed = jnp.dot(wo1[j], att1[:, t], preferred_element_type=f32)
                b = jnp.concatenate([bo1[j]] * (step_tokens // 128), axis=1)
                before = x1[quart((y % 2) * 2 + j), t].astype(f32)
                res[j, :, t] = (summed + b + before).astype(bf16)
            r_copy(s).start()
            out[:, t] = res[c, :, t]
            return carry

        lax.fori_loop(0, STEPS, last, 0)
        for s in range(STEPS):
            r_copy(s).wait_send()
            h_copy(0, s, mate).wait_send()

    @pl.when(jnp.logical_not(at_home))
    def _():
        for s in range(STEPS):
            h_copy(0, s, near).wait_send()
            h_copy(1, s, across).wait_send()
            r_copy(s).wait_recv()

    for s in range(STEPS):
        for j in range(2):
            x_fwd(j, s).wait_send()
            a_fwd(j, s).wait_send()
    for ch in range(CHUNKS):
        x_send_to(0, ch, other).wait_send()
        x_send_to(1, ch, other).wait_send()
        a_copy(0, ch).wait_send()
        a_copy(1, ch).wait_send()
    for cp in wo0_own() + wo0_fwd():
        cp.wait_send()

    @pl.when(c == home)
    def _():
        for layer in range(BLOCKS):
            w_give(layer).wait_send()

    @pl.when(c != home)
    def _():
        for cp in wo1_copies():
            cp.wait_send()
        for ch in range(CHUNKS):
            x_send_to(2, ch, other).wait_send()

    for layer in range(BLOCKS):
        @pl.when(frame < frames - 1)
        def _():
            for s in range(STEPS):
                kv_copy(layer, s).wait_send()

        for s in range(STEPS):
            @pl.when(corner)
            def _():
                for i in range(1, RING):
                    lower(layer, s, i, kv0).wait_send()

            @pl.when(c == 0)
            def _():
                core_copy(layer, s).wait_send()
                for i in range(1, RING):
                    @pl.when(jnp.logical_or(k == 0, jnp.logical_or(z > 0, x + i != RING)))
                    def _():
                        spread(layer, s, i, kv0).wait_send()

            @pl.when(frame == 0)
            def _():
                for i in range(1, RING):
                    deal(layer, s, i).wait_send()


def shards(tokens, norm_gain, w_qkv, w_out, out_bias):
    rows, qw = tokens.shape[1:]
    width = w_qkv.shape[1]
    w = jnp.transpose(w_qkv, (0, 2, 3, 1)).reshape(BLOCKS, 3 * qw, width)
    wo = jnp.swapaxes(w_out, 1, 2)
    any_spec = pl.BlockSpec(memory_space=pl.ANY)
    vmem = pl.BlockSpec(memory_space=pltpu.VMEM)
    dma = pltpu.SemaphoreType.DMA
    result = pl.pallas_call(
        kernel,
        out_shape=jax.ShapeDtypeStruct((qw, rows), bf16),
        in_specs=[any_spec, vmem, any_spec, any_spec, vmem],
        out_specs=vmem,
        scratch_shapes=[
            pltpu.VMEM((width, rows), bf16),
            pltpu.VMEM((width, rows), bf16),
            pltpu.VMEM((BLOCKS, 3 * qw, width), bf16),
            pltpu.VMEM((width, width), bf16),
            pltpu.VMEM((width, 128), f32),
            pltpu.VMEM((2, qw, width), bf16),
            pltpu.VMEM((2, qw, 128), f32),
            pltpu.VMEM((rows, 384), bf16),
            pltpu.VMEM((BLOCKS, 2 * qw, rows), bf16),
            pltpu.VMEM((BLOCKS, 2 * qw, rows), bf16),
            pltpu.VMEM((BLOCKS, 2 * qw, rows), bf16),
            pltpu.VMEM((width, rows), bf16),
            pltpu.VMEM((width, rows), bf16),
            pltpu.VMEM((2, qw, rows), bf16),
            pltpu.VMEM((HEADS, rows, 128), f32),
            pltpu.VMEM((HEADS, rows, 128), f32),
            pltpu.VMEM((HEADS, rows, 128), f32),
            pltpu.VMEM((BLOCKS, width, 128), f32),
            pltpu.VMEM((BLOCKS, qw, 128), f32),
            dma((3, CHUNKS)), dma((2, STEPS)), dma((4, CHUNKS)), dma((2,)), dma((2,)),
            dma((5,)), dma((10,)), dma((5,)), dma((6,)),
            dma((BLOCKS, STEPS)), dma((BLOCKS, STEPS)),
            dma((BLOCKS, STEPS, 4)), dma((BLOCKS, STEPS)), dma((BLOCKS, STEPS, 4)),
            dma((BLOCKS, STEPS, 4)), dma((BLOCKS, STEPS, 4)),
            dma((BLOCKS, STEPS)), dma((BLOCKS, STEPS)), dma((BLOCKS, STEPS)),
            dma((2, CHUNKS)), dma((2, STEPS)), dma((4, CHUNKS)),
            dma((2, STEPS)), dma((4, STEPS)), dma((STEPS,)), dma((STEPS,)),
        ],
        compiler_params=pltpu.CompilerParams(
            collective_id=0, has_side_effects=True, vmem_limit_bytes=60 << 20
        ),
        name="video_blocks",
    )(jnp.swapaxes(tokens[0], 0, 1), norm_gain, w, wo, out_bias)
    return jnp.swapaxes(result, 0, 1)[None]


def solution(mesh):
    placed = (
        P("frame", None, "head"),
        P(),
        P(None, None, None, "head"),
        P(None, None, "head"),
        P(None, "head"),
    )
    return jax.shard_map(
        shards, mesh=mesh, in_specs=placed, out_specs=P("frame", None, "head"), check_vma=False
    )
```

```python
import functools

import jax
import jax.numpy as jnp
from jax import lax
from jax.experimental import pallas as pl
from jax.experimental.pallas import tpu as pltpu
from jax.sharding import PartitionSpec as P

HEAD_DIM = 64
BLOCKS = 2
HEADS = 5
CHUNKS = 8
STEPS = 4
HALVES = 2
RING = 4
MESH = pl.DeviceIdType.MESH
f32 = jnp.float32
bf16 = jnp.bfloat16
SCALE = HEAD_DIM**-0.5 * 1.4426950408889634


def rcopy(src, dst, send, recv, device):
    return pltpu.make_async_remote_copy(
        src_ref=src,
        dst_ref=dst,
        send_sem=send,
        recv_sem=recv,
        device_id=device,
        device_id_type=MESH,
    )


def kernel(
    tok, gain, w, wo, bias, out,
    xg, x1, wbuf, wo0, bo0, wo1, bo1, q_s, kv, kvp, kv0, attg, att1, res, acc_s, m_s, l_s, gcol, bcol,
    x_send, xf_send, x_recv, w_send, w_recv, o_send, o_recv, b_send, b_recv,
    kv_send, kv_recv, q_send, q_recv, d_send, z_send, z_recv, t_recv, c_send, c_recv, a_send, af_send, a_recv, h_send, h_recv, r_send, r_recv,
):
    qw, tokens = tok.shape
    width = gain.shape[1]
    cr = tokens // CHUNKS
    step_tokens = tokens // STEPS
    half_tokens = tokens // HALVES
    zr = 2 * qw // RING
    f = lax.axis_index("frame")
    h = lax.axis_index("head")
    k, y, c = f // 2, (f % 2) * 2 + h // 2, h % 2
    x, z = k // RING, k % RING
    frames = lax.axis_size("frame")
    frame = 2 * k + c
    home = y // 2
    rel = (y - 2 * c + RING) % RING

    def quarter(yy, cc):
        return (yy % 2) * 2 + cc

    def group_of(yy):
        return (yy % 2) * 2 + yy // 2

    def dev(kk, yy, cc):
        return (kk * 2 + yy // 2, (yy % 2) * 2 + cc)

    q_own = quarter(y, c)
    group = group_of(y)
    yp, ym, yo = (y + 1) % RING, (y + RING - 1) % RING, (y + 2) % RING
    g_m, g_p, g_o = group_of(ym), group_of(yp), group_of(yo)
    other = dev(k, y, 1 - c)
    ks = frames // 2
    far = dev((k + jnp.where(c == 1, 1, ks - 1)) % ks, y, 1 - c)
    target = dev(((frame + 1) % frames) // 2, y, 1 - c)

    barrier = pltpu.get_barrier_semaphore()
    friends = [
        other, far, dev(k, yo, c),
        dev(k, yp, 0), dev(k, yp, 1), dev(k, ym, 0), dev(k, ym, 1),
    ]
    for d in friends:
        pl.semaphore_signal(barrier, inc=1, device_id=d, device_id_type=MESH)

    def along_x(i):
        return dev((x + i) % RING * RING + z, y, 0)

    def along_z(i):
        return dev(x * RING + (z + i) % RING, y, 0)

    @pl.when(c == 0)
    def _():
        for i in range(1, RING):
            for d in (along_x(i), along_z(i)):
                pl.semaphore_signal(barrier, inc=1, device_id=d, device_id_type=MESH)

    pl.semaphore_wait(barrier, len(friends) + 2 * (RING - 1) * (1 - c))

    def span(i, size):
        return pl.ds(i * size if isinstance(i, int) else pl.multiple_of(i * size, size), size)

    def quart(q, size=None):
        return span(q, qw if size is None else size)

    def x_send_to(i, ch, device):
        t = span(ch, cr)
        return rcopy(
            tok.at[:, t], xg.at[quart(q_own), t], x_send.at[i, ch], x_recv.at[q_own, ch], device
        )

    def x_wait(q, ch):
        part = xg.at[quart(q), span(ch, cr)]
        rcopy(part, part, x_send.at[0, 0], x_recv.at[q, ch], other).wait_recv()

    plus = jnp.logical_or(rel == 1, rel == 2)
    off = jnp.where(plus, 0, 1)
    fpair = 2 * (1 - rel % 2)
    fdev = dev(k, jnp.where(plus, yp, ym), c)

    def x_fwd(j, s):
        part = xg.at[quart(fpair + j), span(2 * s + off, cr)]
        return rcopy(part, part, xf_send.at[j, s], x_recv.at[fpair + j, 2 * s + off], fdev)

    def x_local(ch):
        t = span(ch, cr)
        return pltpu.make_async_copy(tok.at[:, t], xg.at[quart(q_own), t], x_recv.at[q_own, ch])

    def x_issue(s):
        a, b = 2 * s, 2 * s + 1
        x_send_to(0, a, dev(k, yp, home)).start()
        x_send_to(1, b, dev(k, ym, home)).start()
        x_send_to(0, b, dev(k, yp, home)).start()
        x_send_to(1, a, dev(k, ym, home)).start()

        @pl.when(c == home)
        def _():
            x_local(a).start()
            x_local(b).start()

        @pl.when(c != home)
        def _():
            x_send_to(2, a, other).start()
            x_send_to(2, b, other).start()

    def w_local(layer):
        return pltpu.make_async_copy(w.at[layer], wbuf.at[layer], w_recv.at[layer])

    def w_give(layer):
        return rcopy(w.at[layer], wbuf.at[layer], w_send.at[layer], w_recv.at[layer], other)

    def w_wait(layer):
        rcopy(wbuf.at[layer], wbuf.at[layer], w_send.at[0], w_recv.at[layer], other).wait_recv()

    def wo1_copies():
        return (
            rcopy(wo.at[1], wo1.at[c], o_send.at[4], o_recv.at[8 + c], other),
            rcopy(bcol.at[1], bo1.at[c], b_send.at[4], b_recv.at[4 + c], other),
        )

    hw = qw // 2

    def wo0_part(i, src, row, size, recv, device):
        return rcopy(src, wo0.at[pl.ds(row, size)], o_send.at[i], o_recv.at[recv], device)

    def bo0_part(i, src, q, device):
        return rcopy(src, bo0.at[quart(q)], b_send.at[i], b_recv.at[q], device)

    def mult(v):
        return pl.multiple_of(v, 32)

    def wo0_own():
        base = q_own * qw
        return (
            wo0_part(0, wo.at[0], mult(base), qw, 2 * q_own, other),
            wo0_part(1, wo.at[0, pl.ds(0, hw)], mult(base), hw, 2 * q_own, dev(k, ym, c)),
            wo0_part(
                2, wo.at[0, pl.ds(hw, hw)], mult(base + hw), hw, 2 * q_own + 1, dev(k, yp, c)
            ),
            bo0_part(0, bcol.at[0], q_own, other),
            bo0_part(1, bcol.at[0], q_own, dev(k, ym, c)),
        )

    q_next = quarter(yp, c)
    q_last = quarter(yp, 1 - c)

    def wo0_fwd():
        return (
            wo0_part(3, wo0.at[quart(q_next)], mult(q_next * qw), qw, 2 * q_next, other),
            bo0_part(2, bo0.at[quart(q_next)], q_next, other),
        )

    def wo0_wait(q, size, recv):
        part = wo0.at[pl.ds(mult(q * qw), size)]
        rcopy(part, part, o_send.at[0], o_recv.at[recv], other).wait_recv()

    def bo0_wait(q):
        bo0_part(0, bo0.at[quart(q)], q, other).wait_recv()

    def ln_qkv(layer, src, s):
        t = span(s, step_tokens)
        wide = step_tokens // 128
        total = 0.0
        for q in range(4):
            total += jnp.sum(src[quart(q), t].astype(f32), 0, keepdims=True)
        mean = total * (1.0 / width)
        total = 0.0
        for q in range(4):
            d = src[quart(q), t].astype(f32) - mean
            total += jnp.sum(d * d, 0, keepdims=True)
        inv = lax.rsqrt(total * (1.0 / width) + 1e-5)
        normed = []
        for q in range(4):
            g = gcol[layer, quart(q), :]
            d = src[quart(q), t].astype(f32) - mean
            normed.append((d * inv * jnp.concatenate([g] * wide, axis=1)).astype(bf16))
        proj = jnp.dot(
            wbuf[layer], jnp.concatenate(normed, axis=0), preferred_element_type=f32
        )
        kv[layer, :, t] = proj[qw:].astype(bf16)
        for p in range(3):
            rows = proj[128 * p : min(128 * (p + 1), qw)] * SCALE
            if p == 2:
                rows = jnp.concatenate([rows, jnp.zeros_like(rows)], axis=0)
            q_s[t, 128 * p : 128 * (p + 1)] = rows.T.astype(bf16)

    def kv_copy(layer, s):
        t = span(s, step_tokens)
        return rcopy(
            kv.at[layer, :, t], kvp.at[layer, :, t],
            kv_send.at[layer, s], kv_recv.at[layer, s], target,
        )

    corner = jnp.logical_and(c == 0, z == 0)
    inner = jnp.logical_and(c == 0, frame > 0)

    def piece(buf, layer, s, i):
        return buf.at[layer, span(i, zr), span(s, step_tokens)]

    def deal(layer, s, i):
        return rcopy(
            piece(kv, layer, s, i), piece(kv0, layer, s, i),
            q_send.at[layer, s, i], q_recv.at[layer, s], along_x(i),
        )

    def lower(layer, s, i, src):
        return rcopy(
            piece(src, layer, s, x), piece(kv0, layer, s, x),
            d_send.at[layer, s, i], q_recv.at[layer, s], along_z(i),
        )

    def spread(layer, s, i, src):
        return rcopy(
            piece(src, layer, s, x), piece(kv0, layer, s, x),
            z_send.at[layer, s, i], z_recv.at[layer, s, x], along_x(i),
        )

    def piece_wait(layer, s, i, recv):
        part = piece(kv0, layer, s, i)
        rcopy(part, part, q_send.at[layer, s, 0], recv, other).wait_recv()

    def root_copy(layer, s):
        t = span(s, step_tokens)
        return pltpu.make_async_copy(
            kv.at[layer, :, t], kv0.at[layer, :, t], t_recv.at[layer, s]
        )

    def core_copy(layer, s):
        part = kv0.at[layer, :, span(s, step_tokens)]
        return rcopy(part, part, c_send.at[layer, s], c_recv.at[layer, s], other)

    def send_kv(layer, s):
        @pl.when(frame < frames - 1)
        def _():
            kv_copy(layer, s).start()

        @pl.when(frame == 0)
        def _():
            for i in range(1, RING):
                deal(layer, s, i).start()
            for i in range(1, RING):
                lower(layer, s, i, kv).start()
            for i in range(1, RING):
                spread(layer, s, i, kv).start()
            root_copy(layer, s).start()

        if layer == 1:
            @pl.when(frame == 0)
            def _():
                t = span(s, step_tokens)
                pltpu.make_async_copy(
                    kv.at[layer, :, t], kvp.at[layer, :, t], kv_recv.at[layer, s]
                ).start()

    def down(layer, s):
        @pl.when(jnp.logical_and(corner, x > 0))
        def _():
            piece_wait(layer, s, x, q_recv.at[layer, s])
            for i in range(1, RING):
                lower(layer, s, i, kv0).start()

    def share(layer, s):
        @pl.when(jnp.logical_and(c == 0, z > 0))
        def _():
            piece_wait(layer, s, x, q_recv.at[layer, s])

        @pl.when(inner)
        def _():
            for i in range(1, RING):
                @pl.when(jnp.logical_or(z > 0, x + i != RING))
                def _():
                    spread(layer, s, i, kv0).start()

    def hand_over(layer, s):
        @pl.when(frame == 0)
        def _():
            root_copy(layer, s).wait()

        @pl.when(inner)
        def _():
            for i in range(1, RING):
                j = (x + i) % RING
                piece_wait(layer, s, j, z_recv.at[layer, s, j])

        @pl.when(c == 0)
        def _():
            core_copy(layer, s).start()

    def first_ready(layer):
        @pl.when(c == 1)
        def _():
            for s in range(STEPS):
                core_copy(layer, s).wait_recv()

    def flash(layer, keys, cols, t, size, first):
        count = tokens if cols is None else half_tokens
        cols = slice(None) if cols is None else cols
        lane = lax.broadcasted_iota(jnp.int32, (size, 128), 1)
        found = []
        for head in range(HEADS):
            p = head // 2
            qq = q_s[t, 128 * p : 128 * (p + 1)]
            if head < 4:
                qq = jnp.where((lane // 64) == head % 2, qq, jnp.zeros_like(qq))
                kk = keys[layer, 128 * p : 128 * (p + 1), cols]
                values = [keys[layer, qw + 128 * p : qw + 128 * (p + 1), cols]]
            else:
                qq = qq[:, :64]
                kk = keys[layer, 256:qw, cols]
                values = [keys[layer, qw + 256 : 2 * qw, cols], jnp.zeros((64, count), bf16)]
            values = jnp.concatenate(values + [jnp.ones((128, count), bf16)], axis=0)
            scores = jnp.dot(qq, kk, preferred_element_type=f32)
            top = jnp.max(scores, -1, keepdims=True)
            wide = top
            if not first:
                before = m_s[head, t, :]
                top = jnp.maximum(before, top)
                wide = jnp.concatenate([top] * (count // 128), axis=1)
            e = jnp.exp2(scores - wide).astype(bf16)
            o = lax.dot_general(e, values, (((1,), (1,)), ((), ())), preferred_element_type=f32)
            acc, total = o[:, :128], o[:, 128:]
            if not first:
                alpha = jnp.exp2(before - top)
                acc = acc_s[head, t, :] * alpha + acc
                total = l_s[head, t, :] * alpha + total
            found.append((acc, total, jnp.broadcast_to(top, (size, 128))))
        return found, lane

    def update(layer, keys, cols, first, between=None):
        size = half_tokens if between is not None else tokens

        def body(s, carry):
            t = span(s, size)
            found, _ = flash(layer, keys, cols, t, size, first)
            for head, (acc, total, top) in enumerate(found):
                acc_s[head, t, :] = acc
                l_s[head, t, :] = total
                m_s[head, t, :] = top
            if between is not None:
                pl.when(s == 0)(between)
            return carry

        lax.fori_loop(0, tokens // size, body, 0)

    def finish(layer, keys, cols, s, dst):
        t = span(s, step_tokens)
        found, lane = flash(layer, keys, cols, t, step_tokens, False)
        pieces = [acc / total for acc, total, _ in found]
        base = group * qw
        dst[pl.ds(mult(base), 128), t] = jnp.where(lane < 64, pieces[0], pieces[1]).T.astype(bf16)
        dst[pl.ds(mult(base + 128), 128), t] = (
            jnp.where(lane < 64, pieces[2], pieces[3]).T.astype(bf16)
        )
        dst[pl.ds(mult(base + 256), 64), t] = pieces[4].T[:64].astype(bf16)

    def half_cols(part):
        return slice(part * half_tokens, (part + 1) * half_tokens)

    def wait_previous(layer, part):
        for s in range(2 * part, 2 * part + 2):
            kv_copy(layer, s).wait_recv()

    def a_copy(direction, ch):
        part = attg.at[quart(group), span(ch, cr)]
        return rcopy(
            part, part, a_send.at[direction, ch], a_recv.at[group, ch],
            dev(k, yp if direction == 0 else ym, c),
        )

    def a_fwd(direction, s):
        ch = 2 * s + direction
        g = g_m if direction == 0 else g_p
        part = attg.at[quart(g), span(ch, cr)]
        return rcopy(
            part, part, af_send.at[direction, s], a_recv.at[g, ch],
            dev(k, yp if direction == 0 else ym, c),
        )

    def a_wait(g, ch):
        part = attg.at[quart(g), span(ch, cr)]
        rcopy(part, part, a_send.at[0, 0], a_recv.at[g, ch], other).wait_recv()

    def a_forward(s):
        a_wait(g_m, 2 * s)
        a_fwd(0, s).start()
        a_wait(g_p, 2 * s + 1)
        a_fwd(1, s).start()

    at_home = rel < 2
    mate = dev(k, jnp.where(rel == 0, yp, ym), c)
    near = dev(k, jnp.where(rel == 2, ym, yp), c)
    across = dev(k, yo, c)

    def h_copy(i, s, device):
        part = att1.at[quart(group), span(s, step_tokens)]
        return rcopy(part, part, h_send.at[i, s], h_recv.at[group, s], device)

    def h_wait(g, s):
        part = att1.at[quart(g), span(s, step_tokens)]
        rcopy(part, part, h_send.at[0, 0], h_recv.at[g, s], other).wait_recv()

    def r_copy(s):
        t = span(s, step_tokens)
        return rcopy(res.at[1 - c, :, t], out.at[:, t], r_send.at[s], r_recv.at[s], other)

    x_issue(0)
    x_issue(1)

    @pl.when(c == home)
    def _():
        w_local(0).start()
        w_give(0).start()

    def column(row):
        return jnp.broadcast_to(row, (128, row.shape[1])).T

    for layer in range(BLOCKS):
        gcol[layer] = column(gain[layer : layer + 1, :])
        row = bias[layer : layer + 1, :].astype(f32)
        row = jnp.concatenate([row, jnp.zeros((1, 384 - qw), f32)], axis=1)
        bcol[layer] = column(row)[:qw]

    def first(s, carry):
        x_wait(fpair, 2 * s + off)
        x_wait(fpair + 1, 2 * s + off)
        x_fwd(0, s).start()
        x_fwd(1, s).start()

        @pl.when(s < STEPS - 2)
        def _():
            x_issue(s + 2)

        @pl.when(s > 0)
        def _():
            down(0, s - 1)

        @pl.when(s > 1)
        def _():
            share(0, s - 2)

        @pl.when(s == 3)
        def _():
            pltpu.make_async_copy(wo.at[0], wo0.at[quart(q_own)], o_recv.at[2 * q_own]).start()
            pltpu.make_async_copy(bcol.at[0], bo0.at[quart(q_own)], b_recv.at[q_own]).start()
            for cp in wo0_own():
                cp.start()

        x_wait(fpair, 2 * s + 1 - off)
        x_wait(fpair + 1, 2 * s + 1 - off)
        for j in range(2):
            x_wait(2 - fpair + j, 2 * s)
            x_wait(2 - fpair + j, 2 * s + 1)

        @pl.when(s == 0)
        def _():
            w_wait(0)

        ln_qkv(0, xg, s)
        send_kv(0, s)

        return carry

    lax.fori_loop(0, STEPS, first, 0)

    @pl.when(c == home)
    def _():
        w_local(1).start()
        w_give(1).start()
        pltpu.make_async_copy(wo.at[1], wo1.at[c], o_recv.at[8 + c]).start()
        pltpu.make_async_copy(bcol.at[1], bo1.at[c], b_recv.at[4 + c]).start()

    @pl.when(c != home)
    def _():
        for cp in wo1_copies():
            cp.start()

    def pass_on():
        wo0_wait(q_next, hw, 2 * q_next)
        wo0_wait(q_next, hw, 2 * q_next + 1)
        bo0_wait(q_next)
        for cp in wo0_fwd():
            cp.start()

    share(0, 2)

    @pl.when(frame > 0)
    def _():
        wait_previous(0, 0)
        update(0, kvp, half_cols(0), True, lambda: down(0, 3))
        pass_on()

    @pl.when(frame == 0)
    def _():
        acc_s[...] = jnp.zeros(acc_s.shape, f32)
        l_s[...] = jnp.zeros(l_s.shape, f32)
        m_s[...] = jnp.full(m_s.shape, -jnp.inf, f32)

    share(0, 3)

    @pl.when(frame > 0)
    def _():
        wait_previous(0, 1)
        update(0, kvp, half_cols(1), False)

    for s in range(STEPS):
        hand_over(0, s)
    first_ready(0)

    def second0(s, carry):
        finish(0, kv0, None, s, attg)
        a_copy(0, 2 * s).start()
        a_copy(1, 2 * s + 1).start()
        a_copy(0, 2 * s + 1).start()
        a_copy(1, 2 * s).start()

        @pl.when(jnp.logical_and(frame == 0, s == 1))
        def _():
            pass_on()

        @pl.when(s >= 2)
        def _():
            a_forward(s - 2)

        return carry

    lax.fori_loop(0, STEPS, second0, 0)
    for q in (q_own, quarter(y, 1 - c), q_last):
        wo0_wait(q, qw, 2 * q)
        bo0_wait(q)
    w_wait(1)

    def third(s, carry):
        a_wait(g_m, 2 * s + 1)
        a_wait(g_p, 2 * s)
        a_wait(g_o, 2 * s)
        a_wait(g_o, 2 * s + 1)
        t = span(s, step_tokens)
        for q in range(4):
            summed = jnp.dot(wo0[quart(q), :], attg[:, t], preferred_element_type=f32)
            b = jnp.concatenate([bo0[quart(q), :]] * (step_tokens // 128), axis=1)
            x1[quart(q), t] = (summed + b + xg[quart(q), t].astype(f32)).astype(bf16)
        @pl.when(s < STEPS - 2)
        def _():
            a_forward(s + 2)

        ln_qkv(1, x1, s)
        send_kv(1, s)

        down(1, s)

        @pl.when(s > 0)
        def _():
            share(1, s - 1)

        return carry

    lax.fori_loop(0, STEPS, third, 0)

    share(1, 3)
    wait_previous(1, 0)
    update(1, kvp, half_cols(0), True)
    for s in range(STEPS):
        hand_over(1, s)
    first_ready(1)
    update(1, kv0, None, False)
    wait_previous(1, 1)

    def second1(s, carry):
        finish(1, kvp, half_cols(1), s, att1)

        @pl.when(at_home)
        def _():
            h_copy(0, s, mate).start()

        @pl.when(jnp.logical_not(at_home))
        def _():
            h_copy(0, s, near).start()
            h_copy(1, s, across).start()

        return carry

    lax.fori_loop(0, STEPS, second1, 0)

    @pl.when(at_home)
    def _():
        for j in range(2):
            rcopy(wo.at[1], wo1.at[j], o_send.at[0], o_recv.at[8 + j], other).wait_recv()
            rcopy(bcol.at[1], bo1.at[j], b_send.at[0], b_recv.at[4 + j], other).wait_recv()

        def last(s, carry):
            t = span(s, step_tokens)
            for g in (g_m, g_p, g_o):
                h_wait(g, s)
            for j in range(2):
                summed = jnp.dot(wo1[j], att1[:, t], preferred_element_type=f32)
                b = jnp.concatenate([bo1[j]] * (step_tokens // 128), axis=1)
                before = x1[quart((y % 2) * 2 + j), t].astype(f32)
                res[j, :, t] = (summed + b + before).astype(bf16)
            r_copy(s).start()
            out[:, t] = res[c, :, t]
            return carry

        lax.fori_loop(0, STEPS, last, 0)
        for s in range(STEPS):
            r_copy(s).wait_send()
            h_copy(0, s, mate).wait_send()

    @pl.when(jnp.logical_not(at_home))
    def _():
        for s in range(STEPS):
            h_copy(0, s, near).wait_send()
            h_copy(1, s, across).wait_send()
            r_copy(s).wait_recv()

    for s in range(STEPS):
        for j in range(2):
            x_fwd(j, s).wait_send()
            a_fwd(j, s).wait_send()
    for ch in range(CHUNKS):
        x_send_to(0, ch, other).wait_send()
        x_send_to(1, ch, other).wait_send()
        a_copy(0, ch).wait_send()
        a_copy(1, ch).wait_send()
    for cp in wo0_own() + wo0_fwd():
        cp.wait_send()

    @pl.when(c == home)
    def _():
        for layer in range(BLOCKS):
            w_give(layer).wait_send()

    @pl.when(c != home)
    def _():
        for cp in wo1_copies():
            cp.wait_send()
        for ch in range(CHUNKS):
            x_send_to(2, ch, other).wait_send()

    for layer in range(BLOCKS):
        @pl.when(frame < frames - 1)
        def _():
            for s in range(STEPS):
                kv_copy(layer, s).wait_send()

        for s in range(STEPS):
            @pl.when(corner)
            def _():
                for i in range(1, RING):
                    lower(layer, s, i, kv0).wait_send()

            @pl.when(c == 0)
            def _():
                core_copy(layer, s).wait_send()
                for i in range(1, RING):
                    @pl.when(jnp.logical_or(k == 0, jnp.logical_or(z > 0, x + i != RING)))
                    def _():
                        spread(layer, s, i, kv0).wait_send()

            @pl.when(frame == 0)
            def _():
                for i in range(1, RING):
                    deal(layer, s, i).wait_send()


def shards(tokens, norm_gain, w_qkv, w_out, out_bias):
    rows, qw = tokens.shape[1:]
    width = w_qkv.shape[1]
    w = jnp.transpose(w_qkv, (0, 2, 3, 1)).reshape(BLOCKS, 3 * qw, width)
    wo = jnp.swapaxes(w_out, 1, 2)
    any_spec = pl.BlockSpec(memory_space=pl.ANY)
    vmem = pl.BlockSpec(memory_space=pltpu.VMEM)
    dma = pltpu.SemaphoreType.DMA
    result = pl.pallas_call(
        kernel,
        out_shape=jax.ShapeDtypeStruct((qw, rows), bf16),
        in_specs=[any_spec, vmem, any_spec, any_spec, vmem],
        out_specs=vmem,
        scratch_shapes=[
            pltpu.VMEM((width, rows), bf16),
            pltpu.VMEM((width, rows), bf16),
            pltpu.VMEM((BLOCKS, 3 * qw, width), bf16),
            pltpu.VMEM((width, width), bf16),
            pltpu.VMEM((width, 128), f32),
            pltpu.VMEM((2, qw, width), bf16),
            pltpu.VMEM((2, qw, 128), f32),
            pltpu.VMEM((rows, 384), bf16),
            pltpu.VMEM((BLOCKS, 2 * qw, rows), bf16),
            pltpu.VMEM((BLOCKS, 2 * qw, rows), bf16),
            pltpu.VMEM((BLOCKS, 2 * qw, rows), bf16),
            pltpu.VMEM((width, rows), bf16),
            pltpu.VMEM((width, rows), bf16),
            pltpu.VMEM((2, qw, rows), bf16),
            pltpu.VMEM((HEADS, rows, 128), f32),
            pltpu.VMEM((HEADS, rows, 128), f32),
            pltpu.VMEM((HEADS, rows, 128), f32),
            pltpu.VMEM((BLOCKS, width, 128), f32),
            pltpu.VMEM((BLOCKS, qw, 128), f32),
            dma((3, CHUNKS)), dma((2, STEPS)), dma((4, CHUNKS)), dma((2,)), dma((2,)),
            dma((5,)), dma((10,)), dma((5,)), dma((6,)),
            dma((BLOCKS, STEPS)), dma((BLOCKS, STEPS)),
            dma((BLOCKS, STEPS, 4)), dma((BLOCKS, STEPS)), dma((BLOCKS, STEPS, 4)),
            dma((BLOCKS, STEPS, 4)), dma((BLOCKS, STEPS, 4)),
            dma((BLOCKS, STEPS)), dma((BLOCKS, STEPS)), dma((BLOCKS, STEPS)),
            dma((2, CHUNKS)), dma((2, STEPS)), dma((4, CHUNKS)),
            dma((2, STEPS)), dma((4, STEPS)), dma((STEPS,)), dma((STEPS,)),
        ],
        compiler_params=pltpu.CompilerParams(
            collective_id=0, has_side_effects=True, vmem_limit_bytes=60 << 20
        ),
        name="video_blocks",
    )(jnp.swapaxes(tokens[0], 0, 1), norm_gain, w, wo, out_bias)
    return jnp.swapaxes(result, 0, 1)[None]


def solution(mesh):
    placed = (
        P("frame", None, "head"),
        P(),
        P(None, None, None, "head"),
        P(None, None, "head"),
        P(None, "head"),
    )
    return jax.shard_map(
        shards, mesh=mesh, in_specs=placed, out_specs=P("frame", None, "head"), check_vma=False
    )
```
